512 devices in a mesh: group: 16 (over y, core), sub: 32 (over z, x).
Axes of the slice: x: 4, y: 8, z: 8, core: 2. Of those that a mesh axis runs over, the one named last changes fastest.
Arguments:
- right_side: float32 [262144, 128], P(('group', 'sub')), may hold values from -6 to 6
- mass: float32 [512, 512], P(('group', 'sub')), may hold values from 0.05 to 0.5
- block_values: float32 [262144, 512], P(('group', 'sub')), may hold values from 0.000390625 to 0.005859375
- block_cols: int32 [4096, 8], P(('group', 'sub')), may hold values from 0 to 7, as said below
- face_rows: int32 [512, 256], P(('group', 'sub')), may hold values from 0 to 511, as said below
- land_rows: int32 [512, 256], P(('group', 'sub')), may hold values from 0 to 511, as said below
- face_counts: int32 [512, 32], P(('group', 'sub')), may hold values from 0 to 8, as said below
- face_weight: float32 [512, 256], P(('group', 'sub')), may hold values from 0.3 to 3
- local_factor: float32 [262144, 128], P(('group', 'sub')), may hold values from -0.25 to 0.25
- basis: float32 [32768, 512], P(('group', 'sub')), may hold values from -0.25 to 0.25
- coarse_inverse: float32 [2048, 2048], P('sub'), may hold values from -1 to 2.5, as said below
Outputs:
- solution_field: float32 [262144, 128], P(('group', 'sub'))
- residual: float32 [262144, 128], P(('group', 'sub'))
The draws below stay inside these ranges and needn't reach their ends.
Inputs may be any that keep to these rules, and one draw needn't show every extreme that they name: `block_cols`: for each k, the column blocks of a subdomain's 8 block rows are a permutation of 0 to 7. `face_rows`: the 256 entries of a subdomain are distinct local rows. `land_rows`: the 256 entries of a subdomain are distinct local rows. `face_counts`: every subdomain has 8 live slots toward at least one peer. `coarse_inverse`: symmetric positive definite.
All inputs are finite; a program needn't handle non-finite values.
Results may differ from the reference program's by a relative error of at most 0.0003.
Values sent between devices are 32-bit elements; how exact they have to be, the bound alone decides.
No kernel may reach another device: no remote copies, remote signals or barrier semaphores. Data moves between devices by JAX's collectives and lax.ppermute only.
A program may use at most 64 MiB of HBM per device.

```python
import math
import jax
import jax.numpy as jnp
from jax import lax

NB = 8
BLK = 64
NNZB = 8
RHS = 128
F = 8
NC = 64
LF = 128
ITERS = 3
SUBDOMAINS = 512
ROWS_DEV = 512
ROWS = 262144
NBT = 4096
NCT = 2048
SLOTS = 256
N_GROUP = 16
N_SUB = 32


def draw_block_cols(key, part):
    key = jax.random.fold_in(key, 11)
    key_list = jax.random.split(key, SUBDOMAINS * NNZB)
    perms = jax.vmap(lambda single: jax.random.permutation(single, NB))(key_list)
    perms = perms.reshape(SUBDOMAINS, NNZB, NB).astype(jnp.int32)
    return jnp.swapaxes(perms, 1, 2).reshape(NBT, NNZB)


def draw_face_rows(key, part):
    key = jax.random.fold_in(key, 23)
    key_list = jax.random.split(key, SUBDOMAINS)
    chosen = jax.vmap(lambda single: jax.random.permutation(single, ROWS_DEV)[:SLOTS])(key_list)
    return chosen.astype(jnp.int32)


def draw_land_rows(key, part):
    key = jax.random.fold_in(key, 37)
    key_list = jax.random.split(key, SUBDOMAINS)
    chosen = jax.vmap(lambda single: jax.random.permutation(single, ROWS_DEV)[:SLOTS])(key_list)
    return chosen.astype(jnp.int32)


def draw_face_counts(key, part):
    key = jax.random.fold_in(key, 41)
    first, second = jax.random.split(key)
    counts = jax.random.randint(first, (SUBDOMAINS, N_SUB), 0, F + 1).astype(jnp.int32)
    fullest = jax.random.randint(second, (SUBDOMAINS,), 0, N_SUB).astype(jnp.int32)
    peers = jnp.arange(N_SUB, dtype=jnp.int32)
    return jnp.where(peers[None, :] == fullest[:, None], jnp.int32(F), counts)


def draw_coarse_inverse(key, part):
    key = jax.random.fold_in(key, 53)
    first, second = jax.random.split(key)
    noise = jnp.clip(jax.random.normal(first, (NCT, NCT), jnp.float32), -4.0, 4.0)
    sym = (noise + noise.T) * (0.3 / (2.0 * NCT) ** 0.5)
    diagonal = 1.0 + 0.5 * jax.random.uniform(second, (NCT,), jnp.float32)
    return sym + jnp.diag(diagonal)


def levels(own_key, extent, cuts, low, largest):
    factor_of, own = 1.0, jax.random.fold_in(own_key, 6)
    for position, shards_of in cuts:
        draws = jnp.exp(jax.random.uniform(jax.random.fold_in(own, position), (shards_of,), jnp.float32, low / len(cuts), largest / len(cuts)))
        factor_of = factor_of * jnp.repeat(draws, extent[position] // shards_of).reshape([-1 if axis == position else 1 for axis in range(len(extent))])
    return factor_of


def normal_values(key, shape, deviation, reach, cuts=(), kind=jnp.bfloat16):
    entries = jax.random.normal(key, shape, jnp.float32) * deviation
    if len(cuts) > 0:
        entries = levels(key, shape, cuts, -0.22, 0.18) * entries
    return jnp.clip(entries, min=-reach, max=reach).astype(kind)


def setup_inputs(seed: int = 0) -> dict:
    key_of = jax.random.split(jax.random.key(seed), 12)
    return {
        "right_side": normal_values(key_of[0], (ROWS, RHS), 1.0, 6.0, ((0, 512),), jnp.float32),
        "mass": jnp.clip(jnp.exp(math.log(0.5) - 2.3025851 * jax.random.uniform(key_of[1], (SUBDOMAINS, ROWS_DEV), jnp.float32) ** levels(key_of[1], (SUBDOMAINS, ROWS_DEV), ((0, 512),), -0.2, 0.2)), 0.05, 0.5),
        "block_values": jnp.clip(jnp.exp(math.log(0.005859375) - 2.7080502 * jax.random.uniform(key_of[2], (ROWS, NNZB * BLK), jnp.float32) ** levels(key_of[2], (ROWS, NNZB * BLK), ((0, 512),), -0.2, 0.2)), 0.000390625, 0.005859375),
        "block_cols": draw_block_cols(jax.random.fold_in(key_of[11], 71), 0),
        "face_rows": draw_face_rows(jax.random.fold_in(key_of[11], 71), 0),
        "land_rows": draw_land_rows(jax.random.fold_in(key_of[11], 71), 0),
        "face_counts": draw_face_counts(jax.random.fold_in(key_of[11], 71), 0),
        "face_weight": jnp.clip(jnp.exp(math.log(3.0) - 2.3025851 * jax.random.uniform(key_of[7], (SUBDOMAINS, SLOTS), jnp.float32) ** levels(key_of[7], (SUBDOMAINS, SLOTS), ((0, 512),), -0.2, 0.2)), 0.3, 3.0),
        "local_factor": normal_values(key_of[8], (ROWS, LF), (4 * LF) ** -0.5, 0.25, ((0, 512),), jnp.float32),
        "basis": normal_values(key_of[9], (SUBDOMAINS * NC, ROWS_DEV), ROWS_DEV ** -0.5, 0.25, ((0, 512),), jnp.float32),
        "coarse_inverse": draw_coarse_inverse(jax.random.fold_in(key_of[11], 71), 0),
    }


highest = lax.Precision.HIGHEST


def swap_peers(sent):
    shaped = sent.reshape((N_GROUP, N_SUB, N_SUB, F) + sent.shape[2:])
    turned = jnp.swapaxes(shaped, 1, 2)
    return turned.reshape((SUBDOMAINS, SLOTS) + sent.shape[2:])


def degree_one(values_dev, cols_dev, faces_dev, lands_dev, weights_dev, received_dev):
    row_total = jnp.sum(values_dev, axis=1)
    col_part = jnp.sum(values_dev.reshape(NB, BLK, NNZB * BLK), axis=1).reshape(NB * NNZB, BLK)
    col_total = jnp.zeros((NB, BLK), jnp.float32).at[cols_dev.reshape(-1)].add(col_part).reshape(ROWS_DEV)
    total = row_total + col_total
    return total.at[faces_dev].add(weights_dev).at[lands_dev].add(received_dev)


def local_one(packed):
    values_dev, cols_dev, field, faces_dev, lands_dev, weights_dev, got_out, got_back, diag_dev = packed
    values_r = values_dev.reshape(NB, BLK, NNZB * BLK)
    blocks = field.reshape(NB, BLK, RHS)
    picked = blocks[cols_dev].reshape(NB, NNZB * BLK, RHS)
    forward = jnp.einsum('rik,rkc->ric', values_r, picked, precision=highest).reshape(ROWS_DEV, RHS)
    back_terms = jnp.einsum('rik,ric->rkc', values_r, blocks, precision=highest).reshape(NB * NNZB, BLK, RHS)
    backward = jnp.zeros((NB, BLK, RHS), jnp.float32).at[cols_dev.reshape(-1)].add(back_terms).reshape(ROWS_DEV, RHS)
    coupled = jnp.zeros((ROWS_DEV, RHS), jnp.float32).at[lands_dev].add(got_out)
    coupled = coupled.at[faces_dev].add(weights_dev[:, None] * got_back)
    return diag_dev[:, None] * field - forward - backward - coupled


def reference(right_side, mass, block_values, block_cols, face_rows, land_rows, face_counts, face_weight, local_factor, basis, coarse_inverse):
    values_all = block_values.reshape(SUBDOMAINS, ROWS_DEV, NNZB * BLK)
    cols_all = block_cols.reshape(SUBDOMAINS, NB, NNZB)
    slot_ids = jnp.arange(SLOTS)
    live = (slot_ids % F)[None, :] < face_counts[:, slot_ids // F]
    weights = jnp.where(live, face_weight, jnp.float32(0.0))
    received = swap_peers(weights)
    degree = jax.vmap(degree_one)(values_all, cols_all, face_rows, land_rows, weights, received)
    diag = mass + degree
    factor_r = local_factor.reshape(SUBDOMAINS, ROWS_DEV // LF, LF, LF)
    basis_r = basis.reshape(SUBDOMAINS, NC, ROWS_DEV)

    def operate(field):
        sent_out = weights[:, :, None] * jnp.take_along_axis(field, face_rows[:, :, None], axis=1)
        sent_back = jnp.take_along_axis(field, land_rows[:, :, None], axis=1)
        got_out = swap_peers(sent_out)
        got_back = swap_peers(sent_back)
        return lax.map(local_one, (values_all, cols_all, field, face_rows, land_rows, weights, got_out, got_back, diag))

    def precondition(resid):
        jacobi = resid / diag[:, :, None]
        blocks = resid.reshape(SUBDOMAINS, ROWS_DEV // LF, LF, RHS)
        inner = jnp.einsum('dbij,dbjc->dbic', factor_r, blocks, precision=highest)
        local_part = jnp.einsum('dbji,dbjc->dbic', factor_r, inner, precision=highest).reshape(SUBDOMAINS, ROWS_DEV, RHS)
        coarse_part = jnp.einsum('dnr,drc->dnc', basis_r, resid, precision=highest)
        coarse_rhs = jnp.sum(coarse_part.reshape(N_GROUP, NCT, RHS), axis=0)
        solved = jnp.dot(coarse_inverse, coarse_rhs, precision=highest).reshape(N_SUB, NC, RHS)
        spread = jnp.broadcast_to(solved[None], (N_GROUP, N_SUB, NC, RHS)).reshape(SUBDOMAINS, NC, RHS)
        coarse_term = jnp.einsum('dnr,dnc->drc', basis_r, spread, precision=highest)
        return jacobi + local_part + coarse_term

    resid = right_side.reshape(SUBDOMAINS, ROWS_DEV, RHS)
    solution = jnp.zeros_like(resid)
    zvalue = precondition(resid)
    direction = zvalue
    gamma = jnp.sum(resid * zvalue, axis=(0, 1))
    for iteration in range(ITERS):
        image = operate(direction)
        alpha = gamma / jnp.sum(direction * image, axis=(0, 1))
        solution = solution + alpha * direction
        resid = resid - alpha * image
        if iteration + 1 < ITERS:
            zvalue = precondition(resid)
            gamma_new = jnp.sum(resid * zvalue, axis=(0, 1))
            direction = zvalue + (gamma_new / gamma) * direction
            gamma = gamma_new
    return solution.reshape(ROWS, RHS), resid.reshape(ROWS, RHS)
```

```python
import functools

import jax
import jax.numpy as jnp
from jax import lax
from jax.experimental import pallas as pl
from jax.experimental.pallas import tpu as pltpu
from jax.sharding import PartitionSpec as P

F32, BF16 = jnp.float32, jnp.bfloat16
ROWS, RHS, NC, SLOTS, BLK, NB = 512, 128, 64, 256, 64, 8
N_GROUP, N_SUB, LF = 16, 32, 128
VEC = (ROWS, RHS)
MSG_GROUP = (N_GROUP, 8, 128)
MSG_SUB = (N_SUB, 8, 128)
MSG_FACE = (N_SUB, 16, 128)


def split(x):
    high = x.astype(BF16)
    return high, (x - high.astype(F32)).astype(BF16)


def split3(x):
    high, rest = x.astype(BF16), None
    rest = x - high.astype(F32)
    mid = rest.astype(BF16)
    return high, mid, (rest - mid.astype(F32)).astype(BF16)


def dot(a, b):
    return jnp.dot(a, b, preferred_element_type=F32)


def dot_nt(a, b):
    return lax.dot_general(a, b, (((1,), (1,)), ((), ())), preferred_element_type=F32)


def exact(one_hot, x):
    n = x.shape[1]
    both = dot(one_hot, jnp.concatenate(split(x), axis=1))
    return both[:, :n] + both[:, n:]


def dot3(a_high, a_low, x):
    n = x.shape[1]
    x_high, x_low = split(x)
    both = dot(a_high, jnp.concatenate([x_high, x_low], axis=1))
    return both[:, :n] + (both[:, n:] + dot(a_low, x_high))


def rowdot(a, b):
    return jnp.sum(a * b, axis=0, keepdims=True)


def tile_of(*rows):
    index = lax.broadcasted_iota(jnp.int32, (8, RHS), 0)
    tile = jnp.zeros((8, RHS), F32)
    for at, row in enumerate(rows):
        tile = jnp.where(index == at, row, tile)
    return tile


def pack(coarse, aux):
    whole = jnp.concatenate([coarse, aux, jnp.zeros((56, RHS), F32)], axis=0)
    return whole.T.reshape(MSG_GROUP)


def send_faces(field, pick, weight, msg_ref):
    rows = exact(pick, field)
    msg_ref[:, :8, :] = (rows[:SLOTS] * weight).reshape(N_SUB, 8, RHS)
    msg_ref[:, 8:, :] = rows[SLOTS:].reshape(N_SUB, 8, RHS)


def coupled_of(recv_ref, place, weight):
    out = recv_ref[:, :8, :].reshape(SLOTS, RHS)
    back = recv_ref[:, 8:, :].reshape(SLOTS, RHS) * weight
    return exact(place, jnp.concatenate([out, back], axis=0))


def coarse_of(recv_ref, basis_t):
    turned = recv_ref[...].reshape(128, 128).T
    high, low = split(turned[:NC])
    high, low = high.astype(F32), low.astype(F32)
    stack = jnp.concatenate([high, high, low, jnp.zeros((NC, RHS), F32)], axis=0).astype(BF16)
    return dot(basis_t, stack), turned[NC : NC + 8]


def k_first(right_ref, basis_ref, msg_ref):
    high, low = split(basis_ref[...])
    msg_ref[...] = pack(dot3(high, low, right_ref[...]), jnp.zeros((8, RHS), F32))


def k_slots(faces_ref, lands_ref, counts_ref, weight_ref, pick_ref, place_ref, wcol_ref):
    peer = lax.broadcasted_iota(jnp.int32, (N_SUB, SLOTS), 0)
    slot = lax.broadcasted_iota(jnp.int32, (N_SUB, SLOTS), 1)
    spread = jnp.where(slot // 8 == peer, 1.0, 0.0).astype(BF16)
    counts = jnp.broadcast_to(counts_ref[...].astype(F32), (8, N_SUB)).astype(BF16)
    counts = dot(counts, spread)[:1]
    place_in = (lax.broadcasted_iota(jnp.int32, (1, SLOTS), 1) % 8).astype(F32)
    weights = jnp.where(place_in < counts, weight_ref[...], 0.0)
    wcol_ref[...] = jnp.broadcast_to(weights, (128, SLOTS)).T
    faces, lands = faces_ref[...], lands_ref[...]
    row = lax.broadcasted_iota(jnp.int32, (ROWS, SLOTS), 0)
    place_ref[:, :SLOTS] = jnp.where(row == lands, 1.0, 0.0).astype(BF16)
    place_ref[:, SLOTS:] = jnp.where(row == faces, 1.0, 0.0).astype(BF16)
    lane = lax.broadcasted_iota(jnp.int32, (SLOTS, 128), 1).astype(F32)
    for at, index in enumerate((faces, lands)):
        column = jnp.broadcast_to(index.astype(F32), (128, SLOTS)).T
        for t in range(ROWS // 128):
            pick_ref[at * SLOTS : (at + 1) * SLOTS, t * 128 : (t + 1) * 128] = jnp.where(
                column == lane + float(t * 128), 1.0, 0.0
            ).astype(BF16)


def k_setup(cols_ref, values_ref, mass_ref, bh_ref, bl_ref, base_ref, dense_ref):
    lane = lax.broadcasted_iota(jnp.int32, (1, 128), 1)
    upper = jnp.where(lane >= BLK, 1, 0)
    for b in range(NB):
        rows = slice(b * BLK, (b + 1) * BLK)
        parts = []
        for m in range(NB // 2):
            block = values_ref[rows, m * 128 : (m + 1) * 128]
            first, second = cols_ref[b, 2 * m], cols_ref[b, 2 * m + 1]
            parts.append((block, jnp.where(lane < BLK, first, second) - upper))
            parts.append(
                (pltpu.roll(block, BLK, axis=1), jnp.where(lane < BLK, second, first) - upper)
            )
        for t in range(NB // 2):
            total = None
            for block, column in parts:
                term = block * jnp.where(column == 2 * t, 1.0, 0.0)
                total = term if total is None else total + term
            dense_ref[rows, t * 128 : (t + 1) * 128] = total
    dense = dense_ref[...]
    both = dense + dense.T
    bh_ref[...], bl_ref[...] = split(both)
    mass = jnp.broadcast_to(mass_ref[...], (128, ROWS)).T
    base_ref[...] = mass + jnp.sum(both, axis=1, keepdims=True)


def k_factor(factor_ref, basis_ref, inverse_ref, gh_ref, gl_ref, sh_ref, sl_ref, st_ref, ch_ref, cl_ref):
    for b in range(ROWS // LF):
        rows = slice(b * LF, (b + 1) * LF)
        block = factor_ref[rows, :]
        high, low = split(block.T)
        gh_ref[rows, :], gl_ref[rows, :] = split(dot3(high, low, block))
    high, low = split(basis_ref[...])
    sh_ref[...], sl_ref[...] = high, low
    high, low = high.astype(F32), low.astype(F32)
    st_ref[...] = jnp.concatenate([high, low, high, jnp.zeros((NC, ROWS), F32)], axis=0).T.astype(BF16)
    high, low = split(inverse_ref[...])
    ch_ref[:NC, :], cl_ref[:NC, :] = high, low
    ch_ref[NC:, :] = jnp.zeros((128 - NC, N_SUB * NC), BF16)
    cl_ref[NC:, :] = jnp.zeros((128 - NC, N_SUB * NC), BF16)


def k_gather_first(recv_ref, wcol_ref, msg_ref):
    total = jnp.sum(recv_ref[...], axis=0)
    lane = lax.broadcasted_iota(jnp.int32, MSG_SUB, 2)
    msg_ref[...] = jnp.where(lane == 127, wcol_ref[...].reshape(MSG_SUB), total[None])


def k_gather(recv_ref, msg_ref):
    msg_ref[...] = jnp.broadcast_to(jnp.sum(recv_ref[...], axis=0)[None], MSG_SUB)


def k_solve(recv_ref, ch_ref, cl_ref, msg_ref):
    lane = lax.broadcasted_iota(jnp.int32, (8, 128), 1)
    tiles = []
    aux = jnp.zeros((8, 128), F32)
    for j in range(N_SUB // 2):
        even, odd = recv_ref[2 * j], recv_ref[2 * j + 1]
        tiles.append(jnp.where(lane < NC, even, pltpu.roll(odd, NC, axis=1)))
        aux = aux + (even + odd)
    whole = jnp.concatenate(tiles, axis=1)
    high = whole.astype(BF16).astype(F32)
    stack = jnp.concatenate([high, whole - high], axis=0).astype(BF16)
    first = dot_nt(stack, ch_ref[...])
    solved = first[:8] + (first[8:] + dot_nt(stack, cl_ref[...])[:8])
    tile = jnp.where(lane < NC, solved, aux)
    msg_ref[...] = jnp.broadcast_to(tile[None], MSG_GROUP)


def k_diag(recv_ref, place_ref, wcol_ref, base_ref, diag_ref, inv_ref):
    lane = lax.broadcasted_iota(jnp.int32, (SLOTS, 128), 1)
    got = jnp.where(lane == 127, recv_ref[...].reshape(SLOTS, 128), 0.0)
    got = jnp.broadcast_to(jnp.sum(got, axis=1, keepdims=True), (SLOTS, 128))
    both = jnp.concatenate([got, wcol_ref[...]], axis=0)
    diag = base_ref[...]
    for part in split3(both):
        diag = diag + dot(place_ref[...], part)
    diag_ref[...] = diag
    inv_ref[...] = 1.0 / diag


def k_smooth(field_ref, inv_ref, gh_ref, gl_ref, out_ref):
    for b in range(ROWS // LF):
        rows = slice(b * LF, (b + 1) * LF)
        field = field_ref[rows, :]
        out_ref[rows, :] = field * inv_ref[rows, :] + dot3(gh_ref[rows, :], gl_ref[rows, :], field)


def k_start(recv_ref, smooth_ref, st_ref, pick_ref, wcol_ref, z_ref, msg_ref):
    coarse, _ = coarse_of(recv_ref, st_ref[...])
    z = smooth_ref[...] + coarse
    z_ref[...] = z
    send_faces(z, pick_ref[...], wcol_ref[...], msg_ref)


def k_local0(z_ref, right_ref, diag_ref, bh_ref, bl_ref, out_ref, dots_ref):
    z = z_ref[...]
    out_ref[...] = diag_ref[...] * z - dot3(bh_ref[...], bl_ref[...], z)
    dots_ref[...] = tile_of(rowdot(right_ref[...], z))


def k_image(recv_ref, local_ref, z_ref, dots_ref, place_ref, wcol_ref, sh_ref, sl_ref, image_ref, msg_ref):
    image = local_ref[...] - coupled_of(recv_ref, place_ref[...], wcol_ref[...])
    image_ref[...] = image
    index = lax.broadcasted_iota(jnp.int32, (8, RHS), 0)
    aux = jnp.where(index == 2, rowdot(z_ref[...], image), dots_ref[...])
    msg_ref[...] = pack(dot3(sh_ref[...], sl_ref[...], image), aux)


def k_step0(recv_ref, smooth_ref, z_ref, st_ref, pick_ref, wcol_ref, u_ref, znew_ref, scal_ref, msg_ref):
    coarse, aux = coarse_of(recv_ref, st_ref[...])
    gamma, pap = aux[0:1], aux[2:3]
    alpha = gamma / pap
    u = smooth_ref[...] + coarse
    u_ref[...] = u
    znew = z_ref[...] - alpha * u
    znew_ref[...] = znew
    scal_ref[...] = tile_of(alpha, gamma, pap)
    send_faces(znew, pick_ref[...], wcol_ref[...], msg_ref)


def k_local1(z_ref, right_ref, q_ref, scal_ref, diag_ref, bh_ref, bl_ref, out_ref, resid_ref, dots_ref):
    z, q = z_ref[...], q_ref[...]
    out_ref[...] = diag_ref[...] * z - dot3(bh_ref[...], bl_ref[...], z)
    resid = right_ref[...] - scal_ref[0:1] * q
    resid_ref[...] = resid
    dots_ref[...] = tile_of(rowdot(resid, z), rowdot(z, q))


def k_step1(
    recv_ref, smooth_ref, u_ref, z_ref, scal_ref, st_ref, pick_ref, wcol_ref, znew_ref, scalnew_ref, msg_ref
):
    coarse, aux = coarse_of(recv_ref, st_ref[...])
    gamma, cross, zaz = aux[0:1], aux[1:2], aux[2:3]
    beta = gamma / scal_ref[1:2]
    pap = zaz + beta * (2.0 * cross + beta * scal_ref[2:3])
    alpha = gamma / pap
    u = smooth_ref[...] + coarse + beta * u_ref[...]
    znew = z_ref[...] - alpha * u
    znew_ref[...] = znew
    scalnew_ref[...] = tile_of(alpha, gamma, pap, beta)
    send_faces(znew, pick_ref[...], wcol_ref[...], msg_ref)


def k_local2(
    z_ref, z1_ref, z0_ref, v1_ref, q0_ref, resid_ref, scal0_ref, scal_ref, diag_ref, bh_ref, bl_ref,
    out_ref, direction_ref, image_ref, x_ref, residnew_ref, dots_ref,
):
    z, z0 = z_ref[...], z0_ref[...]
    out_ref[...] = diag_ref[...] * z - dot3(bh_ref[...], bl_ref[...], z)
    alpha, beta = scal_ref[0:1], scal_ref[3:4]
    direction = z1_ref[...] + beta * z0
    image = v1_ref[...] + beta * q0_ref[...]
    direction_ref[...], image_ref[...] = direction, image
    x_ref[...] = scal0_ref[0:1] * z0 + alpha * direction
    resid = resid_ref[...] - alpha * image
    residnew_ref[...] = resid
    dots_ref[...] = tile_of(rowdot(resid, z), rowdot(z, image))


def k_last_image(recv_ref, local_ref, z_ref, dots_ref, place_ref, wcol_ref, image_ref, msg_ref):
    image = local_ref[...] - coupled_of(recv_ref, place_ref[...], wcol_ref[...])
    image_ref[...] = image
    index = lax.broadcasted_iota(jnp.int32, (8, RHS), 0)
    aux = jnp.where(index == 2, rowdot(z_ref[...], image), dots_ref[...])
    msg_ref[...] = jnp.broadcast_to(aux[None], MSG_GROUP)


def k_end(recv_ref, scal_ref, z_ref, v_ref, direction_ref, image_ref, x_ref, resid_ref, xout_ref, rout_ref):
    aux = jnp.sum(recv_ref[...], axis=0)
    gamma, cross, zaz = aux[0:1], aux[1:2], aux[2:3]
    beta = gamma / scal_ref[1:2]
    pap = zaz + beta * (2.0 * cross + beta * scal_ref[2:3])
    alpha = gamma / pap
    xout_ref[...] = x_ref[...] + alpha * (z_ref[...] + beta * direction_ref[...])
    rout_ref[...] = resid_ref[...] - alpha * (v_ref[...] + beta * image_ref[...])


def call(kernel, outs, *args, smem=0, scratch=(), flops=1e6):
    specs = [pl.BlockSpec(memory_space=pltpu.SMEM)] * smem
    specs += [pl.BlockSpec(memory_space=pltpu.VMEM)] * (len(args) - smem)
    single = not isinstance(outs, list)
    shapes = [jax.ShapeDtypeStruct(s, d) for s, d in ([outs] if single else outs)]
    moved = sum(a.size * a.dtype.itemsize for a in [*args, *shapes])
    out = pl.pallas_call(
        kernel,
        out_shape=shapes,
        in_specs=specs,
        out_specs=[pl.BlockSpec(memory_space=pltpu.VMEM)] * len(shapes),
        scratch_shapes=list(scratch),
        compiler_params=pltpu.CompilerParams(vmem_limit_bytes=24 << 20),
        cost_estimate=pl.CostEstimate(flops=int(flops), bytes_accessed=int(moved), transcendentals=0),
    )(*args)
    return out[0] if single else out


def swap(x, axis):
    return lax.all_to_all(x, axis, split_axis=0, concat_axis=0, tiled=True)


def local(
    right_side,
    mass,
    block_values,
    block_cols,
    face_rows,
    land_rows,
    face_counts,
    face_weight,
    local_factor,
    basis,
    coarse_inverse,
):
    vec = (VEC, F32)
    tile = ((8, RHS), F32)
    to_group, to_sub, to_face = (MSG_GROUP, F32), (MSG_SUB, F32), (MSG_FACE, F32)
    square = ((ROWS, ROWS), BF16)

    part = swap(call(k_first, to_group, right_side, basis), "group")
    pick, place, wcol = call(
        k_slots, [square, square, ((SLOTS, 128), F32)], face_rows, land_rows, face_counts, face_weight
    )
    whole = swap(call(k_gather_first, to_sub, part, wcol), "sub")
    gh, gl, sh, sl, st, ch, cl = call(
        k_factor,
        [((ROWS, LF), BF16)] * 2
        + [((NC, ROWS), BF16)] * 2
        + [((ROWS, 256), BF16)]
        + [((128, N_SUB * NC), BF16)] * 2,
        local_factor,
        basis,
        coarse_inverse,
    )
    bh, bl, base = call(
        k_setup,
        [square, square, vec],
        block_cols,
        block_values,
        mass,
        smem=1,
        scratch=[pltpu.VMEM((ROWS, ROWS), F32)],
    )
    solved = swap(call(k_solve, to_group, whole, ch, cl), "group")
    diag, inv = call(k_diag, [vec, vec], whole, place, wcol, base)

    def smooth(field):
        return call(k_smooth, vec, field, inv, gh, gl)

    def coarse(msg):
        whole = swap(call(k_gather, to_sub, swap(msg, "group")), "sub")
        return swap(call(k_solve, to_group, whole, ch, cl), "group")

    def image(msg, near, z, dots):
        return call(k_image, [vec, to_group], swap(msg, "sub"), near, z, dots, place, wcol, sh, sl)

    z0, msg = call(k_start, [vec, to_face], solved, smooth(right_side), st, pick, wcol)
    near, dots = call(k_local0, [vec, tile], z0, right_side, diag, bh, bl)
    q0, msg = image(msg, near, z0, dots)

    solved = coarse(msg)
    u0, z1, scal0, msg = call(
        k_step0, [vec, vec, tile, to_face], solved, smooth(q0), z0, st, pick, wcol
    )
    near, resid1, dots = call(
        k_local1, [vec, vec, tile], z1, right_side, q0, scal0, diag, bh, bl
    )
    v1, msg = image(msg, near, z1, dots)

    solved = coarse(msg)
    z2, scal1, msg = call(
        k_step1, [vec, tile, to_face], solved, smooth(v1), u0, z1, scal0, st, pick, wcol
    )
    near, direction, im, x, resid2, dots = call(
        k_local2, [vec] * 5 + [tile], z2, z1, z0, v1, q0, resid1, scal0, scal1, diag, bh, bl
    )
    v2, msg = call(k_last_image, [vec, to_group], swap(msg, "sub"), near, z2, dots, place, wcol)
    whole = swap(call(k_gather, to_sub, swap(msg, "group")), "sub")
    return tuple(call(k_end, [vec, vec], whole, scal1, z2, v2, direction, im, x, resid2))


def solution(mesh):
    both = P(("group", "sub"), None)
    return jax.shard_map(
        local,
        mesh=mesh,
        in_specs=(both,) * 10 + (P("sub", None),),
        out_specs=(both, both),
        check_vma=False,
    )
```

```python
import functools

import jax
import jax.numpy as jnp
from jax import lax
from jax.experimental import pallas as pl
from jax.experimental.pallas import tpu as pltpu
from jax.sharding import PartitionSpec as P

F32, BF16 = jnp.float32, jnp.bfloat16
ROWS, RHS, NC, SLOTS, BLK, NB = 512, 128, 64, 256, 64, 8
N_GROUP, N_SUB, LF = 16, 32, 128
VEC = (ROWS, RHS)
MSG_GROUP = (N_GROUP, 8, 128)
MSG_SUB = (N_SUB, 8, 128)
MSG_FACE = (N_SUB, 16, 128)


def split(x):
    high = x.astype(BF16)
    return high, (x - high.astype(F32)).astype(BF16)


def split3(x):
    high, rest = x.astype(BF16), None
    rest = x - high.astype(F32)
    mid = rest.astype(BF16)
    return high, mid, (rest - mid.astype(F32)).astype(BF16)


def dot(a, b):
    return jnp.dot(a, b, preferred_element_type=F32)


def dot_nt(a, b):
    return lax.dot_general(a, b, (((1,), (1,)), ((), ())), preferred_element_type=F32)


def exact(one_hot, x):
    n = x.shape[1]
    both = dot(one_hot, jnp.concatenate(split(x), axis=1))
    return both[:, :n] + both[:, n:]


def dot3(a_high, a_low, x):
    n = x.shape[1]
    x_high, x_low = split(x)
    both = dot(a_high, jnp.concatenate([x_high, x_low], axis=1))
    return both[:, :n] + (both[:, n:] + dot(a_low, x_high))


def rowdot(a, b):
    return jnp.sum(a * b, axis=0, keepdims=True)


def tile_of(*rows):
    index = lax.broadcasted_iota(jnp.int32, (8, RHS), 0)
    tile = jnp.zeros((8, RHS), F32)
    for at, row in enumerate(rows):
        tile = jnp.where(index == at, row, tile)
    return tile


def pack(coarse, aux):
    whole = jnp.concatenate([coarse, aux, jnp.zeros((56, RHS), F32)], axis=0)
    return whole.T.reshape(MSG_GROUP)


def one_hot(same):
    return jnp.where(same, 1.0, 0.0).astype(BF16)


def pick_of(columns):
    lane = lax.broadcasted_iota(jnp.int32, (SLOTS, ROWS), 1).astype(F32)
    return jnp.concatenate([one_hot(columns[:, i : i + 1] == lane) for i in range(2)], axis=0)


def place_of(rows):
    row = lax.broadcasted_iota(jnp.int32, (ROWS, SLOTS), 0).astype(F32)
    return jnp.concatenate([one_hot(rows[i : i + 1] == row) for i in (1, 0)], axis=1)


def send_faces(field, columns_ref, msg_ref):
    columns = columns_ref[...]
    rows = exact(pick_of(columns), field)
    msg_ref[:, :8, :] = (rows[:SLOTS] * columns[:, 2:3]).reshape(N_SUB, 8, RHS)
    msg_ref[:, 8:, :] = rows[SLOTS:].reshape(N_SUB, 8, RHS)


def coupled_of(recv_ref, rows_ref, columns_ref):
    out = recv_ref[:, :8, :].reshape(SLOTS, RHS)
    back = recv_ref[:, 8:, :].reshape(SLOTS, RHS) * columns_ref[:, 2:3]
    return exact(place_of(rows_ref[...]), jnp.concatenate([out, back], axis=0))


def coarse_of(recv_ref, basis_t):
    turned = recv_ref[...].reshape(128, 128).T
    high, low = split(turned[:NC])
    high, low = high.astype(F32), low.astype(F32)
    stack = jnp.concatenate([high, high, low, jnp.zeros((NC, RHS), F32)], axis=0).astype(BF16)
    return dot(basis_t, stack), turned[NC : NC + 8]


def k_first(right_ref, basis_ref, msg_ref):
    high, low = split(basis_ref[...])
    msg_ref[...] = pack(dot3(high, low, right_ref[...]), jnp.zeros((8, RHS), F32))


def k_slots(faces_ref, lands_ref, counts_ref, weight_ref, rows_ref, columns_ref):
    peer = lax.broadcasted_iota(jnp.int32, (N_SUB, SLOTS), 0)
    slot = lax.broadcasted_iota(jnp.int32, (N_SUB, SLOTS), 1)
    spread = one_hot(slot // 8 == peer)
    counts = jnp.broadcast_to(counts_ref[...].astype(F32), (8, N_SUB)).astype(BF16)
    counts = dot(counts, spread)[:1]
    place_in = (lax.broadcasted_iota(jnp.int32, (1, SLOTS), 1) % 8).astype(F32)
    weights = jnp.where(place_in < counts, weight_ref[...], 0.0)
    index = lax.broadcasted_iota(jnp.int32, (8, SLOTS), 0)
    rows = jnp.where(index == 2, weights, 0.0)
    rows = jnp.where(index == 0, faces_ref[...].astype(F32), rows)
    rows = jnp.where(index == 1, lands_ref[...].astype(F32), rows)
    rows_ref[...] = rows
    columns_ref[...] = jnp.concatenate([rows, jnp.zeros((120, SLOTS), F32)], axis=0).T


def k_setup(cols_ref, values_ref, mass_ref, bh_ref, bl_ref, base_ref, dense_ref):
    lane = lax.broadcasted_iota(jnp.int32, (1, 128), 1)
    upper = jnp.where(lane >= BLK, 1, 0)
    for b in range(NB):
        rows = slice(b * BLK, (b + 1) * BLK)
        parts = []
        for m in range(NB // 2):
            block = values_ref[rows, m * 128 : (m + 1) * 128]
            first, second = cols_ref[b, 2 * m], cols_ref[b, 2 * m + 1]
            parts.append((block, jnp.where(lane < BLK, first, second) - upper))
            parts.append(
                (pltpu.roll(block, BLK, axis=1), jnp.where(lane < BLK, second, first) - upper)
            )
        for t in range(NB // 2):
            total = None
            for block, column in parts:
                term = block * jnp.where(column == 2 * t, 1.0, 0.0)
                total = term if total is None else total + term
            dense_ref[rows, t * 128 : (t + 1) * 128] = total
    dense = dense_ref[...]
    both = dense + dense.T
    bh_ref[...], bl_ref[...] = split(both)
    mass = jnp.broadcast_to(mass_ref[...], (128, ROWS)).T
    base_ref[...] = mass + jnp.sum(both, axis=1, keepdims=True)


def k_factor(factor_ref, gh_ref, gl_ref):
    for b in range(ROWS // LF):
        rows = slice(b * LF, (b + 1) * LF)
        block = factor_ref[rows, :]
        high, low = split(block.T)
        gh_ref[rows, :], gl_ref[rows, :] = split(dot3(high, low, block))


def k_coarse(basis_ref, inverse_ref, sh_ref, sl_ref, st_ref, ch_ref, cl_ref):
    high, low = split(basis_ref[...])
    sh_ref[...], sl_ref[...] = high, low
    high, low = high.astype(F32), low.astype(F32)
    st_ref[...] = jnp.concatenate([high, low, high, jnp.zeros((NC, ROWS), F32)], axis=0).T.astype(BF16)
    ch_ref[...], cl_ref[...] = split(inverse_ref[...])


def k_gather_first(recv_ref, columns_ref, msg_ref):
    total = jnp.sum(recv_ref[...], axis=0)
    lane = lax.broadcasted_iota(jnp.int32, MSG_SUB, 2)
    weight = jnp.broadcast_to(columns_ref[:, 2:3], (SLOTS, 128)).reshape(MSG_SUB)
    msg_ref[...] = jnp.where(lane == 127, weight, total[None])


def k_gather(recv_ref, msg_ref):
    msg_ref[...] = jnp.broadcast_to(jnp.sum(recv_ref[...], axis=0)[None], MSG_SUB)


def k_solve(recv_ref, ch_ref, cl_ref, msg_ref):
    lane = lax.broadcasted_iota(jnp.int32, (8, 128), 1)
    tiles = []
    aux = jnp.zeros((8, 128), F32)
    for j in range(N_SUB // 2):
        even, odd = recv_ref[2 * j], recv_ref[2 * j + 1]
        tiles.append(jnp.where(lane < NC, even, pltpu.roll(odd, NC, axis=1)))
        aux = aux + (even + odd)
    whole = jnp.concatenate(tiles, axis=1)
    high = whole.astype(BF16).astype(F32)
    stack = jnp.concatenate([high, whole - high], axis=0).astype(BF16)
    first = dot_nt(stack, ch_ref[...])
    solved = first[:8] + (first[8:] + dot_nt(stack, cl_ref[...])[:8])
    tile = jnp.where(lane < NC, jnp.concatenate([solved, solved], axis=1), aux)
    msg_ref[...] = jnp.broadcast_to(tile[None], MSG_GROUP)


def k_diag(recv_ref, rows_ref, columns_ref, base_ref, diag_ref):
    lane = lax.broadcasted_iota(jnp.int32, (SLOTS, 128), 1)
    got = jnp.where(lane == 127, recv_ref[...].reshape(SLOTS, 128), 0.0)
    got = jnp.broadcast_to(jnp.sum(got, axis=1, keepdims=True), (SLOTS, 128))
    both = jnp.concatenate([got, jnp.broadcast_to(columns_ref[:, 2:3], (SLOTS, 128))], axis=0)
    diag, place = base_ref[...], place_of(rows_ref[...])
    for part in split3(both):
        diag = diag + dot(place, part)
    diag_ref[...] = diag


def k_smooth(field_ref, diag_ref, gh_ref, gl_ref, out_ref):
    for b in range(ROWS // LF):
        rows = slice(b * LF, (b + 1) * LF)
        field = field_ref[rows, :]
        out_ref[rows, :] = field / diag_ref[rows, :] + dot3(gh_ref[rows, :], gl_ref[rows, :], field)


def k_start(recv_ref, smooth_ref, st_ref, columns_ref, z_ref, msg_ref):
    coarse, _ = coarse_of(recv_ref, st_ref[...])
    z = smooth_ref[...] + coarse
    z_ref[...] = z
    send_faces(z, columns_ref, msg_ref)


def k_local0(z_ref, right_ref, diag_ref, bh_ref, bl_ref, out_ref, dots_ref):
    z = z_ref[...]
    out_ref[...] = diag_ref[...] * z - dot3(bh_ref[...], bl_ref[...], z)
    dots_ref[...] = tile_of(rowdot(right_ref[...], z))


def k_image(recv_ref, local_ref, z_ref, dots_ref, rows_ref, columns_ref, sh_ref, sl_ref, image_ref, msg_ref):
    image = local_ref[...] - coupled_of(recv_ref, rows_ref, columns_ref)
    image_ref[...] = image
    index = lax.broadcasted_iota(jnp.int32, (8, RHS), 0)
    aux = jnp.where(index == 2, rowdot(z_ref[...], image), dots_ref[...])
    msg_ref[...] = pack(dot3(sh_ref[...], sl_ref[...], image), aux)


def k_step0(recv_ref, smooth_ref, z_ref, st_ref, columns_ref, u_ref, znew_ref, scal_ref, msg_ref):
    coarse, aux = coarse_of(recv_ref, st_ref[...])
    gamma, pap = aux[0:1], aux[2:3]
    alpha = gamma / pap
    u = smooth_ref[...] + coarse
    u_ref[...] = u
    znew = z_ref[...] - alpha * u
    znew_ref[...] = znew
    scal_ref[...] = tile_of(alpha, gamma, pap)
    send_faces(znew, columns_ref, msg_ref)


def k_local1(z_ref, right_ref, q_ref, scal_ref, diag_ref, bh_ref, bl_ref, out_ref, resid_ref, dots_ref):
    z, q = z_ref[...], q_ref[...]
    out_ref[...] = diag_ref[...] * z - dot3(bh_ref[...], bl_ref[...], z)
    resid = right_ref[...] - scal_ref[0:1] * q
    resid_ref[...] = resid
    dots_ref[...] = tile_of(rowdot(resid, z), rowdot(z, q))


def k_step1(
    recv_ref, smooth_ref, u_ref, z_ref, scal_ref, st_ref, columns_ref, znew_ref, scalnew_ref, msg_ref
):
    coarse, aux = coarse_of(recv_ref, st_ref[...])
    gamma, cross, zaz = aux[0:1], aux[1:2], aux[2:3]
    beta = gamma / scal_ref[1:2]
    pap = zaz + beta * (2.0 * cross + beta * scal_ref[2:3])
    alpha = gamma / pap
    u = smooth_ref[...] + coarse + beta * u_ref[...]
    znew = z_ref[...] - alpha * u
    znew_ref[...] = znew
    scalnew_ref[...] = tile_of(alpha, gamma, pap, beta)
    send_faces(znew, columns_ref, msg_ref)


def k_local2(
    z_ref, z1_ref, z0_ref, v1_ref, q0_ref, resid_ref, scal0_ref, scal_ref, diag_ref, bh_ref, bl_ref,
    out_ref, direction_ref, image_ref, x_ref, residnew_ref, dots_ref,
):
    z, z0 = z_ref[...], z0_ref[...]
    out_ref[...] = diag_ref[...] * z - dot3(bh_ref[...], bl_ref[...], z)
    alpha, beta = scal_ref[0:1], scal_ref[3:4]
    direction = z1_ref[...] + beta * z0
    image = v1_ref[...] + beta * q0_ref[...]
    direction_ref[...], image_ref[...] = direction, image
    x_ref[...] = scal0_ref[0:1] * z0 + alpha * direction
    resid = resid_ref[...] - alpha * image
    residnew_ref[...] = resid
    dots_ref[...] = tile_of(rowdot(resid, z), rowdot(z, image))


def k_last_image(recv_ref, local_ref, z_ref, dots_ref, rows_ref, columns_ref, image_ref, msg_ref):
    image = local_ref[...] - coupled_of(recv_ref, rows_ref, columns_ref)
    image_ref[...] = image
    index = lax.broadcasted_iota(jnp.int32, (8, RHS), 0)
    aux = jnp.where(index == 2, rowdot(z_ref[...], image), dots_ref[...])
    msg_ref[...] = jnp.broadcast_to(aux[None], MSG_GROUP)


def k_end(recv_ref, scal_ref, z_ref, v_ref, direction_ref, image_ref, x_ref, resid_ref, xout_ref, rout_ref):
    aux = jnp.sum(recv_ref[...], axis=0)
    gamma, cross, zaz = aux[0:1], aux[1:2], aux[2:3]
    beta = gamma / scal_ref[1:2]
    pap = zaz + beta * (2.0 * cross + beta * scal_ref[2:3])
    alpha = gamma / pap
    xout_ref[...] = x_ref[...] + alpha * (z_ref[...] + beta * direction_ref[...])
    rout_ref[...] = resid_ref[...] - alpha * (v_ref[...] + beta * image_ref[...])


class Far:
    def __init__(self, array):
        self.array = array


def call(kernel, outs, *args, smem=0, scratch=(), flops=1e6, far=False):
    near = pl.BlockSpec(memory_space=pltpu.VMEM)
    specs = [pl.BlockSpec(memory_space=pltpu.SMEM)] * smem
    specs += [pl.BlockSpec() if isinstance(a, Far) else near for a in args[smem:]]
    args = [pltpu.with_memory_space_constraint(a.array, pltpu.HBM) if isinstance(a, Far) else a for a in args]
    single = not isinstance(outs, list)
    sizes = [jax.ShapeDtypeStruct(s, d) for s, d in ([outs] if single else outs)]
    shapes = [pltpu.HBM(a.shape, a.dtype) for a in sizes] if far else sizes
    moved = sum(a.size * a.dtype.itemsize for a in [*args, *sizes])
    out = pl.pallas_call(
        kernel,
        out_shape=shapes,
        in_specs=specs,
        out_specs=[pl.BlockSpec() if far else near] * len(shapes),
        scratch_shapes=list(scratch),
        compiler_params=pltpu.CompilerParams(vmem_limit_bytes=24 << 20),
        cost_estimate=pl.CostEstimate(flops=int(flops), bytes_accessed=int(moved), transcendentals=0),
    )(*args)
    return out[0] if single else out


def swap(x, axis):
    return lax.all_to_all(x, axis, split_axis=0, concat_axis=0, tiled=True)


def local(
    right_side,
    mass,
    block_values,
    block_cols,
    face_rows,
    land_rows,
    face_counts,
    face_weight,
    local_factor,
    basis,
    coarse_inverse,
):
    vec = (VEC, F32)
    tile = ((8, RHS), F32)
    to_group, to_sub, to_face = (MSG_GROUP, F32), (MSG_SUB, F32), (MSG_FACE, F32)
    square = ((ROWS, ROWS), BF16)

    part = swap(call(k_first, to_group, Far(right_side), Far(basis)), "group")
    rows, columns = call(
        k_slots, [((8, SLOTS), F32), ((SLOTS, 128), F32)], face_rows, land_rows, face_counts, face_weight
    )
    whole = swap(call(k_gather_first, to_sub, part, columns), "sub")
    sh, sl, st, ch, cl = call(
        k_coarse,
        [((NC, ROWS), BF16)] * 2 + [((ROWS, 256), BF16)] + [((NC, N_SUB * NC), BF16)] * 2,
        Far(basis),
        Far(coarse_inverse),
    )
    gh, gl = call(k_factor, [((ROWS, LF), BF16)] * 2, Far(local_factor), far=True)
    bh, bl, base = call(
        k_setup,
        [square, square, vec],
        block_cols,
        Far(block_values),
        Far(mass),
        smem=1,
        scratch=[pltpu.VMEM((ROWS, ROWS), F32)],
        far=True,
    )
    gh, gl, bh, bl, base, right = (Far(a) for a in (gh, gl, bh, bl, base, right_side))
    solved = swap(call(k_solve, to_group, whole, ch, cl), "group")
    diag = Far(call(k_diag, vec, whole, rows, columns, base, far=True))

    def smooth(field):
        return call(k_smooth, vec, field, diag, gh, gl)

    def coarse(msg):
        whole = swap(call(k_gather, to_sub, swap(msg, "group")), "sub")
        return swap(call(k_solve, to_group, whole, ch, cl), "group")

    def image(msg, near, z, dots):
        return call(k_image, [vec, to_group], swap(msg, "sub"), near, z, dots, rows, columns, sh, sl)

    z0, msg = call(k_start, [vec, to_face], solved, smooth(right), st, columns)
    near, dots = call(k_local0, [vec, tile], z0, right, diag, bh, bl)
    q0, msg = image(msg, near, z0, dots)

    solved = coarse(msg)
    u0, z1, scal0, msg = call(
        k_step0, [vec, vec, tile, to_face], solved, smooth(q0), z0, st, columns
    )
    near, resid1, dots = call(
        k_local1, [vec, vec, tile], z1, right, q0, scal0, diag, bh, bl
    )
    v1, msg = image(msg, near, z1, dots)

    solved = coarse(msg)
    z2, scal1, msg = call(
        k_step1, [vec, tile, to_face], solved, smooth(v1), u0, z1, scal0, st, columns
    )
    near, direction, im, x, resid2, dots = call(
        k_local2, [vec] * 5 + [tile], z2, z1, z0, v1, q0, resid1, scal0, scal1, diag, bh, bl
    )
    v2, msg = call(k_last_image, [vec, to_group], swap(msg, "sub"), near, z2, dots, rows, columns)
    whole = swap(call(k_gather, to_sub, swap(msg, "group")), "sub")
    return tuple(call(k_end, [vec, vec], whole, scal1, z2, v2, direction, im, x, resid2))


def solution(mesh):
    both = P(("group", "sub"), None)
    return jax.shard_map(
        local,
        mesh=mesh,
        in_specs=(both,) * 10 + (P("sub", None),),
        out_specs=(both, both),
        check_vma=False,
    )
```

```python
import jax
import jax.numpy as jnp
from jax import lax
from jax.experimental import pallas as pl
from jax.experimental.pallas import tpu as pltpu
from jax.sharding import PartitionSpec as P

F32, BF16 = jnp.float32, jnp.bfloat16
ROWS, RHS, NC, SLOTS, BLK, NB = 512, 128, 64, 256, 64, 8
N_GROUP, N_SUB, LF = 16, 32, 128
VEC = (ROWS, RHS)
MSG_GROUP = (N_GROUP, 8, 128)
MSG_SUB = (N_SUB, 8, 128)
MSG_FACE = (N_SUB, 16, 128)
LAST_GROUP, LAST_SUB = (N_GROUP, 4, 128), (N_SUB, 4, 128)


def split(x):
    high = x.astype(BF16)
    rest = x - high.astype(F32)
    mid = rest.astype(BF16)
    return high, mid, (rest - mid.astype(F32)).astype(BF16)


def dot(a, b):
    return jnp.dot(a, b, preferred_element_type=F32)


def dot_nt(a, b):
    return lax.dot_general(a, b, (((1,), (1,)), ((), ())), preferred_element_type=F32)


def folded(products, n):
    total = None
    for at in reversed(range(products.shape[1] // n)):
        part = products[:, at * n : (at + 1) * n]
        total = part if total is None else total + part
    return total


def exact(one_hot, x):
    return folded(dot(one_hot, jnp.concatenate(split(x), axis=1)), x.shape[1])


def times(a, x):
    parts = split(x)
    total = None
    for order, part in reversed(list(enumerate(split(a)))):
        right = jnp.concatenate(parts[: len(parts) - order], axis=1)
        term = folded(dot(part, right), x.shape[1])
        total = term if total is None else total + term
    return total


def rowdot(a, b):
    return jnp.sum(a * b, axis=0, keepdims=True)


def tile_of(*rows):
    index = lax.broadcasted_iota(jnp.int32, (8, RHS), 0)
    tile = jnp.zeros((8, RHS), F32)
    for at, row in enumerate(rows):
        tile = jnp.where(index == at, row, tile)
    return tile


def pack(coarse, aux):
    whole = jnp.concatenate([coarse, aux, jnp.zeros((56, RHS), F32)], axis=0)
    return whole.T.reshape(MSG_GROUP)


def one_hot(same):
    return jnp.where(same, 1.0, 0.0).astype(BF16)


def pick_of(columns):
    lane = lax.broadcasted_iota(jnp.int32, (SLOTS, ROWS), 1).astype(F32)
    return jnp.concatenate([one_hot(columns[:, i : i + 1] == lane) for i in range(2)], axis=0)


def place_of(rows):
    row = lax.broadcasted_iota(jnp.int32, (ROWS, SLOTS), 0).astype(F32)
    return jnp.concatenate([one_hot(rows[i : i + 1] == row) for i in (1, 0)], axis=1)


def send_faces(field, columns_ref, msg_ref):
    columns = columns_ref[...]
    rows = exact(pick_of(columns), field)
    msg_ref[:, :8, :] = (rows[:SLOTS] * columns[:, 2:3]).reshape(N_SUB, 8, RHS)
    msg_ref[:, 8:, :] = rows[SLOTS:].reshape(N_SUB, 8, RHS)


def coupled_of(recv_ref, rows_ref, columns_ref):
    out = recv_ref[:, :8, :].reshape(SLOTS, RHS)
    back = recv_ref[:, 8:, :].reshape(SLOTS, RHS) * columns_ref[:, 2:3]
    return exact(place_of(rows_ref[...]), jnp.concatenate([out, back], axis=0))


def coarse_of(recv_ref, turned_ref):
    turned = recv_ref[...].reshape(128, 128).T
    return times(turned_ref[...], turned[:NC]), turned[NC : NC + 8]


def smooth_of(field_ref, diag_ref, gram_ref):
    parts = []
    for b in range(ROWS // LF):
        rows = slice(b * LF, (b + 1) * LF)
        field = field_ref[rows, :]
        parts.append(field / diag_ref[rows, :] + times(gram_ref[rows, :], field))
    return jnp.concatenate(parts, axis=0)


def k_first(right_ref, basis_ref, msg_ref):
    msg_ref[...] = pack(times(basis_ref[...], right_ref[...]), jnp.zeros((8, RHS), F32))


def k_slots(faces_ref, lands_ref, counts_ref, weight_ref, factor_ref, rows_ref, columns_ref, gram_ref):
    peer = lax.broadcasted_iota(jnp.int32, (N_SUB, SLOTS), 0)
    slot = lax.broadcasted_iota(jnp.int32, (N_SUB, SLOTS), 1)
    spread = one_hot(slot // 8 == peer)
    counts = jnp.broadcast_to(counts_ref[...].astype(F32), (8, N_SUB)).astype(BF16)
    counts = dot(counts, spread)[:1]
    place_in = (lax.broadcasted_iota(jnp.int32, (1, SLOTS), 1) % 8).astype(F32)
    weights = jnp.where(place_in < counts, weight_ref[...], 0.0)
    index = lax.broadcasted_iota(jnp.int32, (8, SLOTS), 0)
    rows = jnp.where(index == 2, weights, 0.0)
    rows = jnp.where(index == 0, faces_ref[...].astype(F32), rows)
    rows = jnp.where(index == 1, lands_ref[...].astype(F32), rows)
    rows_ref[...] = rows
    columns_ref[...] = jnp.concatenate([rows, jnp.zeros((120, SLOTS), F32)], axis=0).T
    for b in range(ROWS // LF):
        at = slice(b * LF, (b + 1) * LF)
        block = factor_ref[at, :]
        gram_ref[at, :] = times(block.T, block)


def k_setup(cols_ref, values_ref, mass_ref, basis_ref, blocks_ref, base_ref, turned_ref, dense_ref):
    lane = lax.broadcasted_iota(jnp.int32, (1, 128), 1)
    upper = jnp.where(lane >= BLK, 1, 0)
    for b in range(NB):
        rows = slice(b * BLK, (b + 1) * BLK)
        parts = []
        for m in range(NB // 2):
            block = values_ref[rows, m * 128 : (m + 1) * 128]
            first, second = cols_ref[b, 2 * m], cols_ref[b, 2 * m + 1]
            parts.append((block, jnp.where(lane < BLK, first, second) - upper))
            parts.append(
                (pltpu.roll(block, BLK, axis=1), jnp.where(lane < BLK, second, first) - upper)
            )
        for t in range(NB // 2):
            total = None
            for block, column in parts:
                term = block * jnp.where(column == 2 * t, 1.0, 0.0)
                total = term if total is None else total + term
            dense_ref[rows, t * 128 : (t + 1) * 128] = total
    dense = dense_ref[...]
    both = dense + dense.T
    blocks_ref[...] = both
    turned_ref[...] = basis_ref[...].T
    mass = jnp.broadcast_to(mass_ref[...], (128, ROWS)).T
    base_ref[...] = mass + jnp.sum(both, axis=1, keepdims=True)


def k_gather_first(recv_ref, columns_ref, msg_ref):
    total = jnp.sum(recv_ref[...], axis=0)
    lane = lax.broadcasted_iota(jnp.int32, MSG_SUB, 2)
    weight = jnp.broadcast_to(columns_ref[:, 2:3], (SLOTS, 128)).reshape(MSG_SUB)
    msg_ref[...] = jnp.where(lane == 127, weight, total[None])


def k_gather(recv_ref, msg_ref):
    msg_ref[...] = jnp.broadcast_to(jnp.sum(recv_ref[...], axis=0)[None], msg_ref.shape)


def k_solve(recv_ref, inverse_ref, msg_ref):
    lane = lax.broadcasted_iota(jnp.int32, (8, 128), 1)
    tiles = []
    aux = jnp.zeros((8, 128), F32)
    for j in range(N_SUB // 2):
        even, odd = recv_ref[2 * j], recv_ref[2 * j + 1]
        tiles.append(jnp.where(lane < NC, even, pltpu.roll(odd, NC, axis=1)))
        aux = aux + (even + odd)
    parts = [part.astype(F32) for part in split(jnp.concatenate(tiles, axis=1))]
    n = len(parts)
    stack = jnp.concatenate(parts + parts[: n % 2], axis=0).astype(BF16)
    solved = None
    for order, part in reversed(list(enumerate(split(inverse_ref[...])))):
        product = dot_nt(stack, part)
        for at in reversed(range(n - order)):
            term = product[at * 8 : (at + 1) * 8]
            solved = term if solved is None else solved + term
    tile = jnp.where(lane < NC, jnp.concatenate([solved, solved], axis=1), aux)
    msg_ref[...] = jnp.broadcast_to(tile[None], MSG_GROUP)


def k_diag(recv_ref, rows_ref, columns_ref, base_ref, diag_ref):
    lane = lax.broadcasted_iota(jnp.int32, (SLOTS, 128), 1)
    got = jnp.where(lane == 127, recv_ref[...].reshape(SLOTS, 128), 0.0)
    got = jnp.broadcast_to(jnp.sum(got, axis=1, keepdims=True), (SLOTS, 128))
    both = jnp.concatenate([got, jnp.broadcast_to(columns_ref[:, 2:3], (SLOTS, 128))], axis=0)
    diag, place = base_ref[...], place_of(rows_ref[...])
    for part in split(both):
        diag = diag + dot(place, part)
    diag_ref[...] = diag


def k_start(recv_ref, right_ref, diag_ref, gram_ref, turned_ref, columns_ref, z_ref, msg_ref):
    coarse, _ = coarse_of(recv_ref, turned_ref)
    z = smooth_of(right_ref, diag_ref, gram_ref) + coarse
    z_ref[...] = z
    send_faces(z, columns_ref, msg_ref)


def k_local0(z_ref, right_ref, diag_ref, blocks_ref, out_ref, dots_ref):
    z = z_ref[...]
    out_ref[...] = diag_ref[...] * z - times(blocks_ref[...], z)
    dots_ref[...] = tile_of(rowdot(right_ref[...], z))


def k_image(recv_ref, local_ref, z_ref, dots_ref, rows_ref, columns_ref, basis_ref, image_ref, msg_ref):
    image = local_ref[...] - coupled_of(recv_ref, rows_ref, columns_ref)
    image_ref[...] = image
    index = lax.broadcasted_iota(jnp.int32, (8, RHS), 0)
    aux = jnp.where(index == 2, rowdot(z_ref[...], image), dots_ref[...])
    msg_ref[...] = pack(times(basis_ref[...], image), aux)


def k_step0(recv_ref, q_ref, diag_ref, gram_ref, z_ref, turned_ref, columns_ref, u_ref, znew_ref, scal_ref, msg_ref):
    coarse, aux = coarse_of(recv_ref, turned_ref)
    gamma, pap = aux[0:1], aux[2:3]
    alpha = gamma / pap
    u = smooth_of(q_ref, diag_ref, gram_ref) + coarse
    u_ref[...] = u
    znew = z_ref[...] - alpha * u
    znew_ref[...] = znew
    scal_ref[...] = tile_of(alpha, gamma, pap)
    send_faces(znew, columns_ref, msg_ref)


def k_local1(z_ref, right_ref, q_ref, scal_ref, diag_ref, blocks_ref, out_ref, resid_ref, dots_ref):
    z, q = z_ref[...], q_ref[...]
    out_ref[...] = diag_ref[...] * z - times(blocks_ref[...], z)
    resid = right_ref[...] - scal_ref[0:1] * q
    resid_ref[...] = resid
    dots_ref[...] = tile_of(rowdot(resid, z), rowdot(z, q))


def k_step1(
    recv_ref, q_ref, diag_ref, gram_ref, u_ref, z_ref, scal_ref, turned_ref, columns_ref, znew_ref, scalnew_ref, msg_ref
):
    coarse, aux = coarse_of(recv_ref, turned_ref)
    gamma, cross, zaz = aux[0:1], aux[1:2], aux[2:3]
    beta = gamma / scal_ref[1:2]
    pap = zaz + beta * (2.0 * cross + beta * scal_ref[2:3])
    alpha = gamma / pap
    u = smooth_of(q_ref, diag_ref, gram_ref) + coarse + beta * u_ref[...]
    znew = z_ref[...] - alpha * u
    znew_ref[...] = znew
    scalnew_ref[...] = tile_of(alpha, gamma, pap, beta)
    send_faces(znew, columns_ref, msg_ref)


def k_local2(
    z_ref, z1_ref, z0_ref, v1_ref, q0_ref, resid_ref, scal0_ref, scal_ref, diag_ref, blocks_ref,
    out_ref, direction_ref, image_ref, x_ref, residnew_ref, dots_ref,
):
    z, z0 = z_ref[...], z0_ref[...]
    out_ref[...] = diag_ref[...] * z - times(blocks_ref[...], z)
    alpha, beta = scal_ref[0:1], scal_ref[3:4]
    direction = z1_ref[...] + beta * z0
    image = v1_ref[...] + beta * q0_ref[...]
    direction_ref[...], image_ref[...] = direction, image
    x_ref[...] = scal0_ref[0:1] * z0 + alpha * direction
    resid = resid_ref[...] - alpha * image
    residnew_ref[...] = resid
    dots_ref[...] = tile_of(rowdot(resid, z), rowdot(z, image))


def k_last_image(recv_ref, local_ref, z_ref, dots_ref, rows_ref, columns_ref, image_ref, msg_ref):
    image = local_ref[...] - coupled_of(recv_ref, rows_ref, columns_ref)
    image_ref[...] = image
    index = lax.broadcasted_iota(jnp.int32, (8, RHS), 0)
    aux = jnp.where(index == 2, rowdot(z_ref[...], image), dots_ref[...])
    msg_ref[...] = jnp.broadcast_to(aux[None, :4], LAST_GROUP)


def k_end(recv_ref, scal_ref, z_ref, v_ref, direction_ref, image_ref, x_ref, resid_ref, xout_ref, rout_ref):
    aux = jnp.sum(recv_ref[...], axis=0)
    gamma, cross, zaz = aux[0:1], aux[1:2], aux[2:3]
    beta = gamma / scal_ref[1:2]
    pap = zaz + beta * (2.0 * cross + beta * scal_ref[2:3])
    alpha = gamma / pap
    xout_ref[...] = x_ref[...] + alpha * (z_ref[...] + beta * direction_ref[...])
    rout_ref[...] = resid_ref[...] - alpha * (v_ref[...] + beta * image_ref[...])


class Far:
    def __init__(self, array):
        self.array = array


def call(kernel, outs, *args, smem=0, scratch=(), flops=1e6, far=()):
    near = pl.BlockSpec(memory_space=pltpu.VMEM)
    specs = [pl.BlockSpec(memory_space=pltpu.SMEM)] * smem
    specs += [pl.BlockSpec() if isinstance(a, Far) else near for a in args[smem:]]
    args = [pltpu.with_memory_space_constraint(a.array, pltpu.HBM) if isinstance(a, Far) else a for a in args]
    single = not isinstance(outs, list)
    sizes = [jax.ShapeDtypeStruct(s, d) for s, d in ([outs] if single else outs)]
    shapes = [pltpu.HBM(a.shape, a.dtype) if i in far else a for i, a in enumerate(sizes)]
    moved = sum(a.size * a.dtype.itemsize for a in [*args, *sizes])
    out = pl.pallas_call(
        kernel,
        out_shape=shapes,
        in_specs=specs,
        out_specs=[pl.BlockSpec() if i in far else near for i in range(len(shapes))],
        scratch_shapes=list(scratch),
        compiler_params=pltpu.CompilerParams(vmem_limit_bytes=24 << 20),
        cost_estimate=pl.CostEstimate(flops=int(flops), bytes_accessed=int(moved), transcendentals=0),
    )(*args)
    return out[0] if single else out


def swap(x, axis):
    return lax.all_to_all(x, axis, split_axis=0, concat_axis=0, tiled=True)


def local(
    right_side,
    mass,
    block_values,
    block_cols,
    face_rows,
    land_rows,
    face_counts,
    face_weight,
    local_factor,
    basis,
    coarse_inverse,
):
    vec = (VEC, F32)
    tile = ((8, RHS), F32)
    to_group, to_sub, to_face = (MSG_GROUP, F32), (MSG_SUB, F32), (MSG_FACE, F32)

    part = swap(call(k_first, to_group, Far(right_side), Far(basis)), "group")
    rows, columns, gram = call(
        k_slots,
        [((8, SLOTS), F32), ((SLOTS, 128), F32), vec],
        face_rows,
        land_rows,
        face_counts,
        face_weight,
        Far(local_factor),
    )
    whole = swap(call(k_gather_first, to_sub, part, columns), "sub")
    blocks, base, turned = call(
        k_setup,
        [((ROWS, ROWS), F32), vec, ((ROWS, NC), F32)],
        block_cols,
        Far(block_values),
        Far(mass),
        Far(basis),
        smem=1,
        scratch=[pltpu.VMEM((ROWS, ROWS), F32)],
        far=(0, 1),
    )
    blocks, right = Far(blocks), Far(right_side)
    first_inverse, turned = lax.optimization_barrier((coarse_inverse, turned))
    solved = swap(call(k_solve, to_group, whole, first_inverse), "group")
    diag = call(k_diag, vec, whole, rows, columns, Far(base))

    def coarse(msg):
        whole = swap(call(k_gather, to_sub, swap(msg, "group")), "sub")
        return swap(call(k_solve, to_group, whole, coarse_inverse), "group")

    def image(msg, near, z, dots):
        return call(k_image, [vec, to_group], swap(msg, "sub"), near, z, dots, rows, columns, basis)

    z0, msg = call(k_start, [vec, to_face], solved, right, diag, gram, turned, columns)
    near, dots = call(k_local0, [vec, tile], z0, right, diag, blocks)
    q0, msg = image(msg, near, z0, dots)

    solved = coarse(msg)
    u0, z1, scal0, msg = call(
        k_step0, [vec, vec, tile, to_face], solved, q0, diag, gram, z0, turned, columns
    )
    near, resid1, dots = call(
        k_local1, [vec, vec, tile], z1, right, q0, scal0, diag, blocks, far=(1,)
    )
    v1, msg = image(msg, near, z1, dots)

    solved = coarse(msg)
    z2, scal1, msg = call(
        k_step1, [vec, tile, to_face], solved, v1, diag, gram, u0, z1, scal0, turned, columns
    )
    near, direction, im, x, resid2, dots = call(
        k_local2, [vec] * 5 + [tile], z2, z1, z0, v1, q0, Far(resid1), scal0, scal1, diag, blocks
    )
    v2, msg = call(
        k_last_image, [vec, (LAST_GROUP, F32)], swap(msg, "sub"), near, z2, dots, rows, columns
    )
    whole = swap(call(k_gather, (LAST_SUB, F32), swap(msg, "group")), "sub")
    return tuple(call(k_end, [vec, vec], whole, scal1, z2, v2, direction, im, x, resid2))


def solution(mesh):
    both = P(("group", "sub"), None)
    return jax.shard_map(
        local,
        mesh=mesh,
        in_specs=(both,) * 10 + (P("sub", None),),
        out_specs=(both, both),
        check_vma=False,
    )
```

```python
import jax
import jax.numpy as jnp
from jax import lax
from jax.experimental import pallas as pl
from jax.experimental.pallas import tpu as pltpu
from jax.sharding import PartitionSpec as P

F32, BF16 = jnp.float32, jnp.bfloat16
ROWS, RHS, NC, SLOTS, BLK, NB = 512, 128, 64, 256, 64, 8
N_GROUP, N_SUB, LF = 16, 32, 128
ORDER = [4 * z + x for x in range(4) for z in range(8)]
PLACE = [ORDER.index(peer) for peer in range(N_SUB)]
VEC = (ROWS, RHS)
MSG_GROUP = (N_GROUP, 8, 128)
MSG_SUB = (N_SUB, 8, 128)
MSG_FACE = (N_SUB, 16, 128)
LAST_GROUP, LAST_SUB = (N_GROUP, 4, 128), (N_SUB, 4, 128)


def split(x):
    high = x.astype(BF16)
    rest = x - high.astype(F32)
    mid = rest.astype(BF16)
    return high, mid, (rest - mid.astype(F32)).astype(BF16)


def dot(a, b):
    return jnp.dot(a, b, preferred_element_type=F32)


def dot_nt(a, b):
    return lax.dot_general(a, b, (((1,), (1,)), ((), ())), preferred_element_type=F32)


def folded(products, n):
    total = None
    for at in reversed(range(products.shape[1] // n)):
        part = products[:, at * n : (at + 1) * n]
        total = part if total is None else total + part
    return total


def exact(one_hot, x):
    return folded(dot(one_hot, jnp.concatenate(split(x), axis=1)), x.shape[1])


def times(a, x):
    parts = split(x)
    total = None
    for order, part in reversed(list(enumerate(split(a)))):
        right = jnp.concatenate(parts[: len(parts) - order], axis=1)
        term = folded(dot(part, right), x.shape[1])
        total = term if total is None else total + term
    return total


def rowdot(a, b):
    return jnp.sum(a * b, axis=0, keepdims=True)


def tile_of(*rows):
    index = lax.broadcasted_iota(jnp.int32, (8, RHS), 0)
    tile = jnp.zeros((8, RHS), F32)
    for at, row in enumerate(rows):
        tile = jnp.where(index == at, row, tile)
    return tile


def pack(coarse, aux):
    whole = jnp.concatenate([coarse, aux, jnp.zeros((56, RHS), F32)], axis=0)
    return whole.T.reshape(MSG_GROUP)


def one_hot(same):
    return jnp.where(same, 1.0, 0.0).astype(BF16)


def pick_of(columns):
    lane = lax.broadcasted_iota(jnp.int32, (SLOTS, ROWS), 1).astype(F32)
    return jnp.concatenate([one_hot(columns[:, i : i + 1] == lane) for i in range(2)], axis=0)


def place_of(rows):
    row = lax.broadcasted_iota(jnp.int32, (ROWS, SLOTS), 0).astype(F32)
    return jnp.concatenate([one_hot(rows[i : i + 1] == row) for i in (1, 0)], axis=1)


def send_faces(field, columns_ref, msg_ref):
    columns = columns_ref[...]
    rows = exact(pick_of(columns), field)
    faces, lands = rows[:SLOTS] * columns[:, 2:3], rows[SLOTS:]
    for at, peer in enumerate(ORDER):
        msg_ref[at, :8, :] = faces[peer * 8 : (peer + 1) * 8]
        msg_ref[at, 8:, :] = lands[peer * 8 : (peer + 1) * 8]


def coupled_of(recv_ref, rows_ref, columns_ref):
    out = jnp.concatenate([recv_ref[at, :8, :] for at in PLACE], axis=0)
    back = jnp.concatenate([recv_ref[at, 8:, :] for at in PLACE], axis=0) * columns_ref[:, 2:3]
    return exact(place_of(rows_ref[...]), jnp.concatenate([out, back], axis=0))


def coarse_of(recv_ref, basis_ref):
    turned = recv_ref[...].reshape(RHS, 128)
    return times(turned[:, :NC], basis_ref[...]).T, turned.T[NC : NC + 8]


def smooth_of(field_ref, smoother_ref):
    blocks = [slice(b * LF, (b + 1) * LF) for b in range(ROWS // LF)]
    return jnp.concatenate([times(smoother_ref[b, :], field_ref[b, :]) for b in blocks], axis=0)


def k_first(right_ref, basis_ref, msg_ref):
    msg_ref[...] = pack(times(basis_ref[...], right_ref[...]), jnp.zeros((8, RHS), F32))


def k_slots(faces_ref, lands_ref, counts_ref, weight_ref, factor_ref, rows_ref, columns_ref, gram_ref):
    peer = lax.broadcasted_iota(jnp.int32, (N_SUB, SLOTS), 0)
    slot = lax.broadcasted_iota(jnp.int32, (N_SUB, SLOTS), 1)
    spread = one_hot(slot // 8 == peer)
    counts = jnp.broadcast_to(counts_ref[...].astype(F32), (8, N_SUB)).astype(BF16)
    counts = dot(counts, spread)[:1]
    place_in = (lax.broadcasted_iota(jnp.int32, (1, SLOTS), 1) % 8).astype(F32)
    weights = jnp.where(place_in < counts, weight_ref[...], 0.0)
    index = lax.broadcasted_iota(jnp.int32, (8, SLOTS), 0)
    rows = jnp.where(index == 2, weights, 0.0)
    rows = jnp.where(index == 0, faces_ref[...].astype(F32), rows)
    rows = jnp.where(index == 1, lands_ref[...].astype(F32), rows)
    rows_ref[...] = rows
    columns_ref[...] = jnp.concatenate([rows, jnp.zeros((120, SLOTS), F32)], axis=0).T
    for b in range(ROWS // LF):
        at = slice(b * LF, (b + 1) * LF)
        block = factor_ref[at, :]
        gram_ref[at, :] = times(block.T, block)


def k_setup(cols_ref, values_ref, mass_ref, blocks_ref, base_ref, dense_ref):
    lane = lax.broadcasted_iota(jnp.int32, (1, 128), 1)
    upper = jnp.where(lane >= BLK, 1, 0)
    for b in range(NB):
        rows = slice(b * BLK, (b + 1) * BLK)
        parts = []
        for m in range(NB // 2):
            block = values_ref[rows, m * 128 : (m + 1) * 128]
            first, second = cols_ref[b, 2 * m], cols_ref[b, 2 * m + 1]
            parts.append((block, jnp.where(lane < BLK, first, second) - upper))
            parts.append(
                (pltpu.roll(block, BLK, axis=1), jnp.where(lane < BLK, second, first) - upper)
            )
        for t in range(NB // 2):
            total = None
            for block, column in parts:
                term = block * jnp.where(column == 2 * t, 1.0, 0.0)
                total = term if total is None else total + term
            dense_ref[rows, t * 128 : (t + 1) * 128] = total
    dense = dense_ref[...]
    both = dense + dense.T
    blocks_ref[...] = both
    mass = jnp.broadcast_to(mass_ref[...], (128, ROWS)).T
    base_ref[...] = mass + jnp.sum(both, axis=1, keepdims=True)


def k_gather_first(recv_ref, columns_ref, msg_ref):
    total = jnp.sum(recv_ref[...], axis=0)
    lane = lax.broadcasted_iota(jnp.int32, (8, 128), 1)
    for at, peer in enumerate(ORDER):
        msg_ref[at] = jnp.where(lane == 127, columns_ref[peer * 8 : (peer + 1) * 8, 2:3], total)


def k_gather(recv_ref, msg_ref):
    msg_ref[...] = jnp.broadcast_to(jnp.sum(recv_ref[...], axis=0)[None], msg_ref.shape)


def k_solve(recv_ref, inverse_ref, msg_ref):
    lane = lax.broadcasted_iota(jnp.int32, (8, 128), 1)
    tiles = []
    aux = jnp.zeros((8, 128), F32)
    for j in range(N_SUB // 2):
        even, odd = recv_ref[PLACE[2 * j]], recv_ref[PLACE[2 * j + 1]]
        tiles.append(jnp.where(lane < NC, even, pltpu.roll(odd, NC, axis=1)))
        aux = aux + (even + odd)
    parts = [part.astype(F32) for part in split(jnp.concatenate(tiles, axis=1))]
    n = len(parts)
    stack = jnp.concatenate(parts + parts[: n % 2], axis=0).astype(BF16)
    solved = None
    for order, part in reversed(list(enumerate(split(inverse_ref[...])))):
        product = dot_nt(stack, part)
        for at in reversed(range(n - order)):
            term = product[at * 8 : (at + 1) * 8]
            solved = term if solved is None else solved + term
    tile = jnp.where(lane < NC, jnp.concatenate([solved, solved], axis=1), aux)
    msg_ref[...] = jnp.broadcast_to(tile[None], MSG_GROUP)


def k_finish(recv_ref, rows_ref, columns_ref, base_ref, blocks_ref, gram_ref, matrix_ref, smoother_ref):
    lane = lax.broadcasted_iota(jnp.int32, (SLOTS, 128), 1)
    got = jnp.concatenate([recv_ref[at] for at in PLACE], axis=0)
    got = jnp.where(lane == 127, got, 0.0)
    got = jnp.broadcast_to(jnp.sum(got, axis=1, keepdims=True), (SLOTS, 128))
    both = jnp.concatenate([got, jnp.broadcast_to(columns_ref[:, 2:3], (SLOTS, 128))], axis=0)
    diag, place = base_ref[...], place_of(rows_ref[...])
    for part in split(both):
        diag = diag + dot(place, part)
    index = lax.broadcasted_iota(jnp.int32, (LF, LF), 0) == lax.broadcasted_iota(jnp.int32, (LF, LF), 1)
    matrix_ref[...] = -blocks_ref[...]
    for b in range(ROWS // LF):
        at = slice(b * LF, (b + 1) * LF)
        matrix_ref[at, at] = jnp.where(index, diag[at], 0.0) - blocks_ref[at, at]
        smoother_ref[at, :] = gram_ref[at, :] + jnp.where(index, 1.0 / diag[at], 0.0)


def k_start(recv_ref, right_ref, smoother_ref, basis_ref, columns_ref, z_ref, msg_ref):
    coarse, _ = coarse_of(recv_ref, basis_ref)
    z = smooth_of(right_ref, smoother_ref) + coarse
    z_ref[...] = z
    send_faces(z, columns_ref, msg_ref)


def image_of(recv_ref, z_ref, matrix_ref, rows_ref, columns_ref):
    return times(matrix_ref[...], z_ref[...]) - coupled_of(recv_ref, rows_ref, columns_ref)


def k_image0(
    recv_ref, z_ref, right_ref, matrix_ref, rows_ref, columns_ref, basis_ref, image_ref, msg_ref
):
    image = image_of(recv_ref, z_ref, matrix_ref, rows_ref, columns_ref)
    image_ref[...] = image
    z = z_ref[...]
    aux = tile_of(rowdot(right_ref[...], z), jnp.zeros((1, RHS), F32), rowdot(z, image))
    msg_ref[...] = pack(times(basis_ref[...], image), aux)


def k_step0(recv_ref, q_ref, smoother_ref, z_ref, basis_ref, columns_ref, u_ref, znew_ref, scal_ref, msg_ref):
    coarse, aux = coarse_of(recv_ref, basis_ref)
    gamma, pap = aux[0:1], aux[2:3]
    alpha = gamma / pap
    u = smooth_of(q_ref, smoother_ref) + coarse
    u_ref[...] = u
    znew = z_ref[...] - alpha * u
    znew_ref[...] = znew
    scal_ref[...] = tile_of(alpha, gamma, pap)
    send_faces(znew, columns_ref, msg_ref)


def k_image1(
    recv_ref, z_ref, right_ref, q_ref, scal_ref, matrix_ref, rows_ref, columns_ref, basis_ref, image_ref, msg_ref
):
    image = image_of(recv_ref, z_ref, matrix_ref, rows_ref, columns_ref)
    image_ref[...] = image
    z, q = z_ref[...], q_ref[...]
    resid = right_ref[...] - scal_ref[0:1] * q
    aux = tile_of(rowdot(resid, z), rowdot(z, q), rowdot(z, image))
    msg_ref[...] = pack(times(basis_ref[...], image), aux)


def k_step1(
    recv_ref, v_ref, smoother_ref, u_ref, z_ref, scal_ref, basis_ref, columns_ref, znew_ref, scalnew_ref, msg_ref
):
    coarse, aux = coarse_of(recv_ref, basis_ref)
    gamma, cross, zaz = aux[0:1], aux[1:2], aux[2:3]
    beta = gamma / scal_ref[1:2]
    pap = zaz + beta * (2.0 * cross + beta * scal_ref[2:3])
    alpha = gamma / pap
    u = smooth_of(v_ref, smoother_ref) + coarse + beta * u_ref[...]
    znew = z_ref[...] - alpha * u
    znew_ref[...] = znew
    scalnew_ref[...] = tile_of(alpha, gamma, pap, beta)
    send_faces(znew, columns_ref, msg_ref)


def second_of(right_ref, q_ref, v_ref, scal0_ref, scal_ref):
    image = v_ref[...] + scal_ref[3:4] * q_ref[...]
    return image, right_ref[...] - scal0_ref[0:1] * q_ref[...] - scal_ref[0:1] * image


def k_image2(
    recv_ref, z_ref, right_ref, q_ref, v_ref, scal0_ref, scal_ref, matrix_ref, rows_ref, columns_ref,
    image_ref, msg_ref,
):
    image = image_of(recv_ref, z_ref, matrix_ref, rows_ref, columns_ref)
    image_ref[...] = image
    z = z_ref[...]
    before, resid = second_of(right_ref, q_ref, v_ref, scal0_ref, scal_ref)
    aux = tile_of(rowdot(resid, z), rowdot(z, before), rowdot(z, image))
    msg_ref[...] = jnp.broadcast_to(aux[None, :4], LAST_GROUP)


def k_end(
    recv_ref, scal0_ref, scal_ref, z0_ref, z1_ref, z2_ref, right_ref, q_ref, v_ref, last_ref, xout_ref, rout_ref
):
    aux = jnp.sum(recv_ref[...], axis=0)
    gamma, cross, zaz = aux[0:1], aux[1:2], aux[2:3]
    beta = gamma / scal_ref[1:2]
    pap = zaz + beta * (2.0 * cross + beta * scal_ref[2:3])
    alpha = gamma / pap
    z0 = z0_ref[...]
    direction = z1_ref[...] + scal_ref[3:4] * z0
    x = scal0_ref[0:1] * z0 + scal_ref[0:1] * direction
    xout_ref[...] = x + alpha * (z2_ref[...] + beta * direction)
    image, resid = second_of(right_ref, q_ref, v_ref, scal0_ref, scal_ref)
    rout_ref[...] = resid - alpha * (last_ref[...] + beta * image)


class Far:
    def __init__(self, array):
        self.array = array


def call(kernel, outs, *args, smem=0, scratch=(), flops=1e6, far=()):
    near = pl.BlockSpec(memory_space=pltpu.VMEM)
    specs = [pl.BlockSpec(memory_space=pltpu.SMEM)] * smem
    specs += [pl.BlockSpec() if isinstance(a, Far) else near for a in args[smem:]]
    args = [pltpu.with_memory_space_constraint(a.array, pltpu.HBM) if isinstance(a, Far) else a for a in args]
    single = not isinstance(outs, list)
    sizes = [jax.ShapeDtypeStruct(s, d) for s, d in ([outs] if single else outs)]
    shapes = [pltpu.HBM(a.shape, a.dtype) if i in far else a for i, a in enumerate(sizes)]
    moved = sum(a.size * a.dtype.itemsize for a in [*args, *sizes])
    out = pl.pallas_call(
        kernel,
        out_shape=shapes,
        in_specs=specs,
        out_specs=[pl.BlockSpec() if i in far else near for i in range(len(shapes))],
        scratch_shapes=list(scratch),
        compiler_params=pltpu.CompilerParams(vmem_limit_bytes=24 << 20),
        cost_estimate=pl.CostEstimate(flops=int(flops), bytes_accessed=int(moved), transcendentals=0),
    )(*args)
    return out[0] if single else out


def swap(x, axis):
    order = [ORDER] if axis == "sub" else None
    return lax.all_to_all(x, axis, split_axis=0, concat_axis=0, tiled=True, axis_index_groups=order)


def local(
    right_side,
    mass,
    block_values,
    block_cols,
    face_rows,
    land_rows,
    face_counts,
    face_weight,
    local_factor,
    basis,
    coarse_inverse,
):
    vec = (VEC, F32)
    tile = ((8, RHS), F32)
    to_group, to_sub, to_face = (MSG_GROUP, F32), (MSG_SUB, F32), (MSG_FACE, F32)

    part = swap(call(k_first, to_group, Far(right_side), Far(basis)), "group")
    rows, columns, gram = call(
        k_slots,
        [((8, SLOTS), F32), ((SLOTS, 128), F32), vec],
        face_rows,
        land_rows,
        face_counts,
        face_weight,
        Far(local_factor),
        far=(2,),
    )
    whole = swap(call(k_gather_first, to_sub, part, columns), "sub")
    blocks, base = call(
        k_setup,
        [((ROWS, ROWS), F32), vec],
        block_cols,
        Far(block_values),
        Far(mass),
        smem=1,
        scratch=[pltpu.VMEM((ROWS, ROWS), F32)],
        far=(0, 1),
    )
    first_inverse, base = lax.optimization_barrier((coarse_inverse, base))
    solved = swap(call(k_solve, to_group, whole, first_inverse), "group")
    matrix, smoother = call(
        k_finish,
        [((ROWS, ROWS), F32), vec],
        whole,
        rows,
        columns,
        Far(base),
        Far(blocks),
        Far(gram),
    )

    def coarse(msg):
        whole = swap(call(k_gather, to_sub, swap(msg, "group")), "sub")
        return swap(call(k_solve, to_group, whole, coarse_inverse), "group")

    z0, msg = call(k_start, [vec, to_face], solved, right_side, smoother, basis, columns)
    q0, msg = call(
        k_image0, [vec, to_group], swap(msg, "sub"), z0, right_side, matrix, rows, columns, basis
    )
    u0, z1, scal0, msg = call(
        k_step0, [vec, vec, tile, to_face], coarse(msg), q0, smoother, z0, basis, columns
    )
    v1, msg = call(
        k_image1,
        [vec, to_group],
        swap(msg, "sub"),
        z1,
        right_side,
        q0,
        scal0,
        matrix,
        rows,
        columns,
        basis,
    )
    z2, scal1, msg = call(
        k_step1, [vec, tile, to_face], coarse(msg), v1, smoother, u0, z1, scal0, basis, columns
    )
    v2, msg = call(
        k_image2,
        [vec, (LAST_GROUP, F32)],
        swap(msg, "sub"),
        z2,
        right_side,
        q0,
        v1,
        scal0,
        scal1,
        matrix,
        rows,
        columns,
    )
    whole = swap(call(k_gather, (LAST_SUB, F32), swap(msg, "group")), "sub")
    return tuple(
        call(k_end, [vec, vec], whole, scal0, scal1, z0, z1, z2, right_side, q0, v1, v2)
    )


def solution(mesh):
    both = P(("group", "sub"), None)
    return jax.shard_map(
        local,
        mesh=mesh,
        in_specs=(both,) * 10 + (P("sub", None),),
        out_specs=(both, both),
        check_vma=False,
    )
```

```python
import jax
import jax.numpy as jnp
from jax import lax
from jax.experimental import pallas as pl
from jax.experimental.pallas import tpu as pltpu
from jax.sharding import PartitionSpec as P

F32, BF16 = jnp.float32, jnp.bfloat16
ROWS, RHS, NC, SLOTS, BLK, NB = 512, 128, 64, 256, 64, 8
N_GROUP, N_SUB, LF = 16, 32, 128
ORDER = [4 * z + x for x in range(4) for z in range(8)]
PLACE = [ORDER.index(peer) for peer in range(N_SUB)]
VEC = (ROWS, RHS)
MSG_GROUP = (N_GROUP, 8, 128)
MSG_SUB = (N_SUB, 8, 128)
MSG_FACE = (N_SUB, 16, 128)
LAST_GROUP, LAST_SUB = (N_GROUP, 4, 128), (N_SUB, 4, 128)


def split(x):
    high = x.astype(BF16)
    rest = x - high.astype(F32)
    mid = rest.astype(BF16)
    return high, mid, (rest - mid.astype(F32)).astype(BF16)


def dot(a, b):
    return jnp.dot(a, b, preferred_element_type=F32)


def dot_nt(a, b):
    return lax.dot_general(a, b, (((1,), (1,)), ((), ())), preferred_element_type=F32)


def folded(products, n):
    total = None
    for at in reversed(range(products.shape[1] // n)):
        part = products[:, at * n : (at + 1) * n]
        total = part if total is None else total + part
    return total


def exact(one_hot, x):
    return folded(dot(one_hot, jnp.concatenate(split(x), axis=1)), x.shape[1])


def times(a, x):
    parts = split(x)
    total = None
    for order, part in reversed(list(enumerate(split(a)))):
        right = jnp.concatenate(parts[: len(parts) - order], axis=1)
        term = folded(dot(part, right), x.shape[1])
        total = term if total is None else total + term
    return total


def rowdot(a, b):
    return jnp.sum(a * b, axis=0, keepdims=True)


def tile_of(*rows):
    index = lax.broadcasted_iota(jnp.int32, (8, RHS), 0)
    tile = jnp.zeros((8, RHS), F32)
    for at, row in enumerate(rows):
        tile = jnp.where(index == at, row, tile)
    return tile


def pack(coarse, aux):
    whole = jnp.concatenate([coarse, aux, jnp.zeros((56, RHS), F32)], axis=0)
    return whole.T.reshape(MSG_GROUP)


def one_hot(same):
    return jnp.where(same, 1.0, 0.0).astype(BF16)


def pick_of(columns):
    lane = lax.broadcasted_iota(jnp.int32, (SLOTS, ROWS), 1).astype(F32)
    return jnp.concatenate([one_hot(columns[:, i : i + 1] == lane) for i in range(2)], axis=0)


def place_of(rows):
    row = lax.broadcasted_iota(jnp.int32, (ROWS, SLOTS), 0).astype(F32)
    return jnp.concatenate([one_hot(rows[i : i + 1] == row) for i in (1, 0)], axis=1)


def send_faces(field, columns_ref, msg_ref):
    columns = columns_ref[...]
    rows = exact(pick_of(columns), field)
    faces, lands = rows[:SLOTS] * columns[:, 2:3], rows[SLOTS:]
    for at, peer in enumerate(ORDER):
        msg_ref[at, :8, :] = faces[peer * 8 : (peer + 1) * 8]
        msg_ref[at, 8:, :] = lands[peer * 8 : (peer + 1) * 8]


def coupled_of(recv_ref, rows_ref, columns_ref):
    out = jnp.concatenate([recv_ref[at, :8, :] for at in PLACE], axis=0)
    back = jnp.concatenate([recv_ref[at, 8:, :] for at in PLACE], axis=0) * columns_ref[:, 2:3]
    return exact(place_of(rows_ref[...]), jnp.concatenate([out, back], axis=0))


def coarse_of(recv_ref, basis_ref):
    turned = recv_ref[...].reshape(RHS, 128)
    return times(turned[:, :NC], basis_ref[...]).T, turned.T[NC : NC + 8]


def smooth_of(field_ref, smoother_ref):
    blocks = [slice(b * LF, (b + 1) * LF) for b in range(ROWS // LF)]
    return jnp.concatenate([times(smoother_ref[b, :], field_ref[b, :]) for b in blocks], axis=0)


def k_first(
    right_ref, basis_ref, faces_ref, lands_ref, counts_ref, weight_ref, msg_ref, rows_ref, columns_ref
):
    msg_ref[...] = pack(times(basis_ref[...], right_ref[...]), jnp.zeros((8, RHS), F32))
    peer = lax.broadcasted_iota(jnp.int32, (N_SUB, SLOTS), 0)
    slot = lax.broadcasted_iota(jnp.int32, (N_SUB, SLOTS), 1)
    spread = one_hot(slot // 8 == peer)
    counts = jnp.broadcast_to(counts_ref[...].astype(F32), (8, N_SUB)).astype(BF16)
    counts = dot(counts, spread)[:1]
    place_in = (lax.broadcasted_iota(jnp.int32, (1, SLOTS), 1) % 8).astype(F32)
    weights = jnp.where(place_in < counts, weight_ref[...], 0.0)
    index = lax.broadcasted_iota(jnp.int32, (8, SLOTS), 0)
    rows = jnp.where(index == 2, weights, 0.0)
    rows = jnp.where(index == 0, faces_ref[...].astype(F32), rows)
    rows = jnp.where(index == 1, lands_ref[...].astype(F32), rows)
    rows_ref[...] = rows
    columns_ref[...] = jnp.concatenate([rows, jnp.zeros((120, SLOTS), F32)], axis=0).T


def k_setup(cols_ref, values_ref, mass_ref, blocks_ref, base_ref, dense_ref):
    lane = lax.broadcasted_iota(jnp.int32, (1, 128), 1)
    upper = jnp.where(lane >= BLK, 1, 0)
    for b in range(NB):
        rows = slice(b * BLK, (b + 1) * BLK)
        parts = []
        for m in range(NB // 2):
            block = values_ref[rows, m * 128 : (m + 1) * 128]
            first, second = cols_ref[b, 2 * m], cols_ref[b, 2 * m + 1]
            parts.append((block, jnp.where(lane < BLK, first, second) - upper))
            parts.append(
                (pltpu.roll(block, BLK, axis=1), jnp.where(lane < BLK, second, first) - upper)
            )
        for t in range(NB // 2):
            total = None
            for block, column in parts:
                term = block * jnp.where(column == 2 * t, 1.0, 0.0)
                total = term if total is None else total + term
            dense_ref[rows, t * 128 : (t + 1) * 128] = total
    dense = dense_ref[...]
    both = dense + dense.T
    blocks_ref[...] = both
    mass = jnp.broadcast_to(mass_ref[...], (128, ROWS)).T
    base_ref[...] = mass + jnp.sum(both, axis=1, keepdims=True)


def k_gather_first(recv_ref, columns_ref, msg_ref):
    total = jnp.sum(recv_ref[...], axis=0)
    lane = lax.broadcasted_iota(jnp.int32, (8, 128), 1)
    for at, peer in enumerate(ORDER):
        msg_ref[at] = jnp.where(lane == 127, columns_ref[peer * 8 : (peer + 1) * 8, 2:3], total)


def k_gather(recv_ref, msg_ref):
    msg_ref[...] = jnp.broadcast_to(jnp.sum(recv_ref[...], axis=0)[None], msg_ref.shape)


def k_solve(recv_ref, inverse_ref, msg_ref):
    lane = lax.broadcasted_iota(jnp.int32, (8, 128), 1)
    tiles = []
    aux = jnp.zeros((8, 128), F32)
    for j in range(N_SUB // 2):
        even, odd = recv_ref[PLACE[2 * j]], recv_ref[PLACE[2 * j + 1]]
        tiles.append(jnp.where(lane < NC, even, pltpu.roll(odd, NC, axis=1)))
        aux = aux + (even + odd)
    parts = [part.astype(F32) for part in split(jnp.concatenate(tiles, axis=1))]
    n = len(parts)
    stack = jnp.concatenate(parts + parts[: n % 2], axis=0).astype(BF16)
    solved = None
    for order, part in reversed(list(enumerate(split(inverse_ref[...])))):
        product = dot_nt(stack, part)
        for at in reversed(range(n - order)):
            term = product[at * 8 : (at + 1) * 8]
            solved = term if solved is None else solved + term
    tile = jnp.where(lane < NC, jnp.concatenate([solved, solved], axis=1), aux)
    msg_ref[...] = jnp.broadcast_to(tile[None], MSG_GROUP)


def k_finish(recv_ref, rows_ref, columns_ref, base_ref, blocks_ref, factor_ref, matrix_ref, smoother_ref):
    lane = lax.broadcasted_iota(jnp.int32, (SLOTS, 128), 1)
    got = jnp.concatenate([recv_ref[at] for at in PLACE], axis=0)
    got = jnp.where(lane == 127, got, 0.0)
    got = jnp.broadcast_to(jnp.sum(got, axis=1, keepdims=True), (SLOTS, 128))
    both = jnp.concatenate([got, jnp.broadcast_to(columns_ref[:, 2:3], (SLOTS, 128))], axis=0)
    diag, place = base_ref[...], place_of(rows_ref[...])
    for part in split(both):
        diag = diag + dot(place, part)
    index = lax.broadcasted_iota(jnp.int32, (LF, LF), 0) == lax.broadcasted_iota(jnp.int32, (LF, LF), 1)
    matrix_ref[...] = -blocks_ref[...]
    for b in range(ROWS // LF):
        at = slice(b * LF, (b + 1) * LF)
        matrix_ref[at, at] = jnp.where(index, diag[at], 0.0) - blocks_ref[at, at]
        factor = factor_ref[at, :]
        smoother_ref[at, :] = times(factor.T, factor) + jnp.where(index, 1.0 / diag[at], 0.0)


def k_start(recv_ref, right_ref, smoother_ref, basis_ref, columns_ref, z_ref, msg_ref):
    coarse, _ = coarse_of(recv_ref, basis_ref)
    z = smooth_of(right_ref, smoother_ref) + coarse
    z_ref[...] = z
    send_faces(z, columns_ref, msg_ref)


def image_of(recv_ref, z_ref, matrix_ref, rows_ref, columns_ref):
    return times(matrix_ref[...], z_ref[...]) - coupled_of(recv_ref, rows_ref, columns_ref)


def k_image0(
    recv_ref, z_ref, right_ref, matrix_ref, rows_ref, columns_ref, basis_ref, image_ref, msg_ref
):
    image = image_of(recv_ref, z_ref, matrix_ref, rows_ref, columns_ref)
    image_ref[...] = image
    z = z_ref[...]
    aux = tile_of(rowdot(right_ref[...], z), jnp.zeros((1, RHS), F32), rowdot(z, image))
    msg_ref[...] = pack(times(basis_ref[...], image), aux)


def k_step0(recv_ref, q_ref, smoother_ref, z_ref, basis_ref, columns_ref, u_ref, znew_ref, scal_ref, msg_ref):
    coarse, aux = coarse_of(recv_ref, basis_ref)
    gamma, pap = aux[0:1], aux[2:3]
    alpha = gamma / pap
    u = smooth_of(q_ref, smoother_ref) + coarse
    u_ref[...] = u
    znew = z_ref[...] - alpha * u
    znew_ref[...] = znew
    scal_ref[...] = tile_of(alpha, gamma, pap)
    send_faces(znew, columns_ref, msg_ref)


def k_image1(
    recv_ref, z_ref, right_ref, q_ref, scal_ref, matrix_ref, rows_ref, columns_ref, basis_ref, image_ref, msg_ref
):
    image = image_of(recv_ref, z_ref, matrix_ref, rows_ref, columns_ref)
    image_ref[...] = image
    z, q = z_ref[...], q_ref[...]
    resid = right_ref[...] - scal_ref[0:1] * q
    aux = tile_of(rowdot(resid, z), rowdot(z, q), rowdot(z, image))
    msg_ref[...] = pack(times(basis_ref[...], image), aux)


def k_step1(
    recv_ref, v_ref, smoother_ref, u_ref, z_ref, scal_ref, basis_ref, columns_ref, znew_ref, scalnew_ref, msg_ref
):
    coarse, aux = coarse_of(recv_ref, basis_ref)
    gamma, cross, zaz = aux[0:1], aux[1:2], aux[2:3]
    beta = gamma / scal_ref[1:2]
    pap = zaz + beta * (2.0 * cross + beta * scal_ref[2:3])
    alpha = gamma / pap
    u = smooth_of(v_ref, smoother_ref) + coarse + beta * u_ref[...]
    znew = z_ref[...] - alpha * u
    znew_ref[...] = znew
    scalnew_ref[...] = tile_of(alpha, gamma, pap, beta)
    send_faces(znew, columns_ref, msg_ref)


def second_of(right_ref, q_ref, v_ref, scal0_ref, scal_ref):
    image = v_ref[...] + scal_ref[3:4] * q_ref[...]
    return image, right_ref[...] - scal0_ref[0:1] * q_ref[...] - scal_ref[0:1] * image


def k_image2(
    recv_ref, z_ref, right_ref, q_ref, v_ref, scal0_ref, scal_ref, matrix_ref, rows_ref, columns_ref,
    image_ref, msg_ref,
):
    image = image_of(recv_ref, z_ref, matrix_ref, rows_ref, columns_ref)
    image_ref[...] = image
    z = z_ref[...]
    before, resid = second_of(right_ref, q_ref, v_ref, scal0_ref, scal_ref)
    aux = tile_of(rowdot(resid, z), rowdot(z, before), rowdot(z, image))
    msg_ref[...] = jnp.broadcast_to(aux[None, :4], LAST_GROUP)


def k_end(
    recv_ref, scal0_ref, scal_ref, z0_ref, z1_ref, z2_ref, right_ref, q_ref, v_ref, last_ref, xout_ref, rout_ref
):
    aux = jnp.sum(recv_ref[...], axis=0)
    gamma, cross, zaz = aux[0:1], aux[1:2], aux[2:3]
    beta = gamma / scal_ref[1:2]
    pap = zaz + beta * (2.0 * cross + beta * scal_ref[2:3])
    alpha = gamma / pap
    z0 = z0_ref[...]
    direction = z1_ref[...] + scal_ref[3:4] * z0
    x = scal0_ref[0:1] * z0 + scal_ref[0:1] * direction
    xout_ref[...] = x + alpha * (z2_ref[...] + beta * direction)
    image, resid = second_of(right_ref, q_ref, v_ref, scal0_ref, scal_ref)
    rout_ref[...] = resid - alpha * (last_ref[...] + beta * image)


class Far:
    def __init__(self, array):
        self.array = array


def call(kernel, outs, *args, smem=0, scratch=(), flops=1e6, far=()):
    near = pl.BlockSpec(memory_space=pltpu.VMEM)
    specs = [pl.BlockSpec(memory_space=pltpu.SMEM)] * smem
    specs += [pl.BlockSpec() if isinstance(a, Far) else near for a in args[smem:]]
    args = [pltpu.with_memory_space_constraint(a.array, pltpu.HBM) if isinstance(a, Far) else a for a in args]
    single = not isinstance(outs, list)
    sizes = [jax.ShapeDtypeStruct(s, d) for s, d in ([outs] if single else outs)]
    shapes = [pltpu.HBM(a.shape, a.dtype) if i in far else a for i, a in enumerate(sizes)]
    moved = sum(a.size * a.dtype.itemsize for a in [*args, *sizes])
    out = pl.pallas_call(
        kernel,
        out_shape=shapes,
        in_specs=specs,
        out_specs=[pl.BlockSpec() if i in far else near for i in range(len(shapes))],
        scratch_shapes=list(scratch),
        compiler_params=pltpu.CompilerParams(vmem_limit_bytes=24 << 20),
        cost_estimate=pl.CostEstimate(flops=int(flops), bytes_accessed=int(moved), transcendentals=0),
    )(*args)
    return out[0] if single else out


def swap(x, axis):
    order = [ORDER] if axis == "sub" else None
    return lax.all_to_all(x, axis, split_axis=0, concat_axis=0, tiled=True, axis_index_groups=order)


def local(
    right_side,
    mass,
    block_values,
    block_cols,
    face_rows,
    land_rows,
    face_counts,
    face_weight,
    local_factor,
    basis,
    coarse_inverse,
):
    vec = (VEC, F32)
    tile = ((8, RHS), F32)
    to_group, to_sub, to_face = (MSG_GROUP, F32), (MSG_SUB, F32), (MSG_FACE, F32)

    part, rows, columns = call(
        k_first,
        [to_group, ((8, SLOTS), F32), ((SLOTS, 128), F32)],
        Far(right_side),
        Far(basis),
        Far(face_rows),
        Far(land_rows),
        Far(face_counts),
        Far(face_weight),
    )
    part = swap(part, "group")
    whole = swap(call(k_gather_first, to_sub, part, columns), "sub")
    blocks, base = call(
        k_setup,
        [((ROWS, ROWS), F32), vec],
        block_cols,
        Far(block_values),
        Far(mass),
        smem=1,
        scratch=[pltpu.VMEM((ROWS, ROWS), F32)],
        far=(0, 1),
    )
    first_inverse, base = lax.optimization_barrier((coarse_inverse, base))
    solved = swap(call(k_solve, to_group, whole, first_inverse), "group")
    matrix, smoother = call(
        k_finish,
        [((ROWS, ROWS), F32), vec],
        whole,
        rows,
        columns,
        Far(base),
        Far(blocks),
        Far(local_factor),
    )

    def coarse(msg):
        whole = swap(call(k_gather, to_sub, swap(msg, "group")), "sub")
        return swap(call(k_solve, to_group, whole, coarse_inverse), "group")

    z0, msg = call(k_start, [vec, to_face], solved, right_side, smoother, basis, columns)
    q0, msg = call(
        k_image0, [vec, to_group], swap(msg, "sub"), z0, right_side, matrix, rows, columns, basis
    )
    u0, z1, scal0, msg = call(
        k_step0, [vec, vec, tile, to_face], coarse(msg), q0, smoother, z0, basis, columns
    )
    v1, msg = call(
        k_image1,
        [vec, to_group],
        swap(msg, "sub"),
        z1,
        right_side,
        q0,
        scal0,
        matrix,
        rows,
        columns,
        basis,
    )
    z2, scal1, msg = call(
        k_step1, [vec, tile, to_face], coarse(msg), v1, smoother, u0, z1, scal0, basis, columns
    )
    v2, msg = call(
        k_image2,
        [vec, (LAST_GROUP, F32)],
        swap(msg, "sub"),
        z2,
        right_side,
        q0,
        v1,
        scal0,
        scal1,
        matrix,
        rows,
        columns,
    )
    whole = swap(call(k_gather, (LAST_SUB, F32), swap(msg, "group")), "sub")
    return tuple(
        call(k_end, [vec, vec], whole, scal0, scal1, z0, z1, z2, right_side, q0, v1, v2)
    )


def solution(mesh):
    both = P(("group", "sub"), None)
    return jax.shard_map(
        local,
        mesh=mesh,
        in_specs=(both,) * 10 + (P("sub", None),),
        out_specs=(both, both),
        check_vma=False,
    )
```

```python
import jax
import jax.numpy as jnp
from jax import lax
from jax.experimental import pallas as pl
from jax.experimental.pallas import tpu as pltpu
from jax.sharding import PartitionSpec as P

F32, BF16 = jnp.float32, jnp.bfloat16
ROWS, RHS, NC, SLOTS, BLK, NB = 512, 128, 64, 256, 64, 8
N_GROUP, N_SUB, LF = 16, 32, 128
ORDER = [4 * z + x for x in range(4) for z in range(8)]
PLACE = [ORDER.index(peer) for peer in range(N_SUB)]
VEC = (ROWS, RHS)
MSG_GROUP = (N_GROUP, 8, 128)
MSG_SUB = (N_SUB, 8, 128)
MSG_FACE = (N_SUB, 16, 128)
LAST_GROUP, LAST_SUB = (N_GROUP, 4, 128), (N_SUB, 4, 128)


def split(x):
    high = x.astype(BF16)
    rest = x - high.astype(F32)
    mid = rest.astype(BF16)
    return high, mid, (rest - mid.astype(F32)).astype(BF16)


def dot(a, b):
    return jnp.dot(a, b, preferred_element_type=F32)


def dot_nt(a, b):
    return lax.dot_general(a, b, (((1,), (1,)), ((), ())), preferred_element_type=F32)


def folded(products, n):
    total = None
    for at in reversed(range(products.shape[1] // n)):
        part = products[:, at * n : (at + 1) * n]
        total = part if total is None else total + part
    return total


def exact(one_hot, x):
    return folded(dot(one_hot, jnp.concatenate(split(x), axis=1)), x.shape[1])


def times(a, x):
    parts = split(x)
    total = None
    for order, part in reversed(list(enumerate(split(a)))):
        right = jnp.concatenate(parts[: len(parts) - order], axis=1)
        term = folded(dot(part, right), x.shape[1])
        total = term if total is None else total + term
    return total


def rowdot(a, b):
    return jnp.sum(a * b, axis=0, keepdims=True)


def tile_of(*rows):
    index = lax.broadcasted_iota(jnp.int32, (8, RHS), 0)
    tile = jnp.zeros((8, RHS), F32)
    for at, row in enumerate(rows):
        tile = jnp.where(index == at, row, tile)
    return tile


def pack(coarse, aux):
    whole = jnp.concatenate([coarse, aux, jnp.zeros((56, RHS), F32)], axis=0)
    return whole.T.reshape(MSG_GROUP)


def one_hot(same):
    return jnp.where(same, 1.0, 0.0).astype(BF16)


def pick_of(columns):
    lane = lax.broadcasted_iota(jnp.int32, (SLOTS, ROWS), 1).astype(F32)
    return jnp.concatenate([one_hot(columns[:, i : i + 1] == lane) for i in range(2)], axis=0)


def place_of(rows):
    row = lax.broadcasted_iota(jnp.int32, (ROWS, SLOTS), 0).astype(F32)
    return jnp.concatenate([one_hot(rows[i : i + 1] == row) for i in (1, 0)], axis=1)


def send_faces(field, columns_ref, msg_ref):
    columns = columns_ref[...]
    rows = exact(pick_of(columns), field)
    faces, lands = rows[:SLOTS] * columns[:, 2:3], rows[SLOTS:]
    for at, peer in enumerate(ORDER):
        msg_ref[at, :8, :] = faces[peer * 8 : (peer + 1) * 8]
        msg_ref[at, 8:, :] = lands[peer * 8 : (peer + 1) * 8]


def arrived(recv_ref, columns_ref):
    out = jnp.concatenate([recv_ref[at, :8, :] for at in PLACE], axis=0)
    back = jnp.concatenate([recv_ref[at, 8:, :] for at in PLACE], axis=0) * columns_ref[:, 2:3]
    return jnp.concatenate([out, back], axis=0)


def coarse_of(recv_ref, basis_ref):
    turned = recv_ref[...].reshape(RHS, 128)
    return times(turned[:, :NC], basis_ref[...]).T, turned.T[NC : NC + 8]


def smooth_of(field_ref, smoother_ref):
    blocks = [slice(b * LF, (b + 1) * LF) for b in range(ROWS // LF)]
    return jnp.concatenate([times(smoother_ref[b, :], field_ref[b, :]) for b in blocks], axis=0)


def k_first(
    right_ref, basis_ref, faces_ref, lands_ref, counts_ref, weight_ref, msg_ref, rows_ref, columns_ref
):
    msg_ref[...] = pack(times(basis_ref[...], right_ref[...]), jnp.zeros((8, RHS), F32))
    peer = lax.broadcasted_iota(jnp.int32, (N_SUB, SLOTS), 0)
    slot = lax.broadcasted_iota(jnp.int32, (N_SUB, SLOTS), 1)
    spread = one_hot(slot // 8 == peer)
    counts = jnp.broadcast_to(counts_ref[...].astype(F32), (8, N_SUB)).astype(BF16)
    counts = dot(counts, spread)[:1]
    place_in = (lax.broadcasted_iota(jnp.int32, (1, SLOTS), 1) % 8).astype(F32)
    weights = jnp.where(place_in < counts, weight_ref[...], 0.0)
    index = lax.broadcasted_iota(jnp.int32, (8, SLOTS), 0)
    rows = jnp.where(index == 2, weights, 0.0)
    rows = jnp.where(index == 0, faces_ref[...].astype(F32), rows)
    rows = jnp.where(index == 1, lands_ref[...].astype(F32), rows)
    rows_ref[...] = rows
    columns_ref[...] = jnp.concatenate([rows, jnp.zeros((120, SLOTS), F32)], axis=0).T


def k_setup(cols_ref, values_ref, mass_ref, blocks_ref, base_ref, dense_ref):
    lane = lax.broadcasted_iota(jnp.int32, (1, 128), 1)
    upper = jnp.where(lane >= BLK, 1, 0)
    for b in range(NB):
        rows = slice(b * BLK, (b + 1) * BLK)
        parts = []
        for m in range(NB // 2):
            block = values_ref[rows, m * 128 : (m + 1) * 128]
            first, second = cols_ref[b, 2 * m], cols_ref[b, 2 * m + 1]
            parts.append((block, jnp.where(lane < BLK, first, second) - upper))
            parts.append(
                (pltpu.roll(block, BLK, axis=1), jnp.where(lane < BLK, second, first) - upper)
            )
        for t in range(NB // 2):
            total = None
            for block, column in parts:
                term = block * jnp.where(column == 2 * t, 1.0, 0.0)
                total = term if total is None else total + term
            dense_ref[rows, t * 128 : (t + 1) * 128] = total
    dense = dense_ref[...]
    both = dense + dense.T
    blocks_ref[...] = both
    mass = jnp.broadcast_to(mass_ref[...], (128, ROWS)).T
    base_ref[...] = mass + jnp.sum(both, axis=1, keepdims=True)


def k_gather_first(recv_ref, columns_ref, msg_ref):
    total = jnp.sum(recv_ref[...], axis=0)
    lane = lax.broadcasted_iota(jnp.int32, (8, 128), 1)
    for at, peer in enumerate(ORDER):
        msg_ref[at] = jnp.where(lane == 127, columns_ref[peer * 8 : (peer + 1) * 8, 2:3], total)


def k_gather(recv_ref, msg_ref):
    msg_ref[...] = jnp.broadcast_to(jnp.sum(recv_ref[...], axis=0)[None], msg_ref.shape)


def k_solve(recv_ref, inverse_ref, msg_ref):
    lane = lax.broadcasted_iota(jnp.int32, (8, 128), 1)
    tiles = []
    aux = jnp.zeros((8, 128), F32)
    for j in range(N_SUB // 2):
        even, odd = recv_ref[PLACE[2 * j]], recv_ref[PLACE[2 * j + 1]]
        tiles.append(jnp.where(lane < NC, even, pltpu.roll(odd, NC, axis=1)))
        aux = aux + (even + odd)
    parts = [part.astype(F32) for part in split(jnp.concatenate(tiles, axis=1))]
    n = len(parts)
    stack = jnp.concatenate(parts + parts[: n % 2], axis=0).astype(BF16)
    solved = None
    for order, part in reversed(list(enumerate(split(inverse_ref[...])))):
        product = dot_nt(stack, part)
        for at in reversed(range(n - order)):
            term = product[at * 8 : (at + 1) * 8]
            solved = term if solved is None else solved + term
    tile = jnp.where(lane < NC, jnp.concatenate([solved, solved], axis=1), aux)
    msg_ref[...] = jnp.broadcast_to(tile[None], MSG_GROUP)


def k_finish(recv_ref, rows_ref, columns_ref, base_ref, blocks_ref, factor_ref, matrix_ref, smoother_ref):
    lane = lax.broadcasted_iota(jnp.int32, (SLOTS, 128), 1)
    got = jnp.concatenate([recv_ref[at] for at in PLACE], axis=0)
    got = jnp.where(lane == 127, got, 0.0)
    got = jnp.broadcast_to(jnp.sum(got, axis=1, keepdims=True), (SLOTS, 128))
    both = jnp.concatenate([got, jnp.broadcast_to(columns_ref[:, 2:3], (SLOTS, 128))], axis=0)
    diag, place = base_ref[...], place_of(rows_ref[...])
    for part in split(both):
        diag = diag + dot(place, part)
    index = lax.broadcasted_iota(jnp.int32, (LF, LF), 0) == lax.broadcasted_iota(jnp.int32, (LF, LF), 1)
    matrix_ref[...] = -blocks_ref[...]
    for b in range(ROWS // LF):
        at = slice(b * LF, (b + 1) * LF)
        matrix_ref[at, at] = jnp.where(index, diag[at], 0.0) - blocks_ref[at, at]
        factor = factor_ref[at, :]
        smoother_ref[at, :] = times(factor.T, factor) + jnp.where(index, 1.0 / diag[at], 0.0)


def k_start(recv_ref, right_ref, smoother_ref, basis_ref, columns_ref, z_ref, msg_ref):
    coarse, _ = coarse_of(recv_ref, basis_ref)
    z = smooth_of(right_ref, smoother_ref) + coarse
    z_ref[...] = z
    send_faces(z, columns_ref, msg_ref)


def image_of(recv_ref, z_ref, matrix_ref, rows_ref, columns_ref):
    high, mid, low = split(matrix_ref[...])
    z = split(z_ref[...])
    got = split(-arrived(recv_ref, columns_ref))
    place = place_of(rows_ref[...])
    pair = jnp.concatenate(z[:2], axis=1)
    right = jnp.concatenate([pair, jnp.concatenate(got[:2], axis=1)], axis=0)
    first = dot(jnp.concatenate([high, place], axis=1), right)
    second = dot(mid, pair)
    left = jnp.concatenate([high, low, place], axis=1)
    third = dot(left, jnp.concatenate([z[2], z[0], got[2]], axis=0))
    return first[:, :RHS] + (first[:, RHS:] + second[:, :RHS] + (second[:, RHS:] + third))


def k_image0(
    recv_ref, z_ref, right_ref, matrix_ref, rows_ref, columns_ref, basis_ref, image_ref, msg_ref
):
    image = image_of(recv_ref, z_ref, matrix_ref, rows_ref, columns_ref)
    image_ref[...] = image
    z = z_ref[...]
    aux = tile_of(rowdot(right_ref[...], z), jnp.zeros((1, RHS), F32), rowdot(z, image))
    msg_ref[...] = pack(times(basis_ref[...], image), aux)


def k_step0(recv_ref, q_ref, smoother_ref, z_ref, basis_ref, columns_ref, u_ref, znew_ref, scal_ref, msg_ref):
    coarse, aux = coarse_of(recv_ref, basis_ref)
    gamma, pap = aux[0:1], aux[2:3]
    alpha = gamma / pap
    u = smooth_of(q_ref, smoother_ref) + coarse
    u_ref[...] = u
    znew = z_ref[...] - alpha * u
    znew_ref[...] = znew
    scal_ref[...] = tile_of(alpha, gamma, pap)
    send_faces(znew, columns_ref, msg_ref)


def k_image1(
    recv_ref, z_ref, right_ref, q_ref, scal_ref, matrix_ref, rows_ref, columns_ref, basis_ref, image_ref, msg_ref
):
    image = image_of(recv_ref, z_ref, matrix_ref, rows_ref, columns_ref)
    image_ref[...] = image
    z, q = z_ref[...], q_ref[...]
    resid = right_ref[...] - scal_ref[0:1] * q
    aux = tile_of(rowdot(resid, z), rowdot(z, q), rowdot(z, image))
    msg_ref[...] = pack(times(basis_ref[...], image), aux)


def k_step1(
    recv_ref, v_ref, smoother_ref, u_ref, z_ref, scal_ref, basis_ref, columns_ref, znew_ref, scalnew_ref, msg_ref
):
    coarse, aux = coarse_of(recv_ref, basis_ref)
    gamma, cross, zaz = aux[0:1], aux[1:2], aux[2:3]
    beta = gamma / scal_ref[1:2]
    pap = zaz + beta * (2.0 * cross + beta * scal_ref[2:3])
    alpha = gamma / pap
    u = smooth_of(v_ref, smoother_ref) + coarse + beta * u_ref[...]
    znew = z_ref[...] - alpha * u
    znew_ref[...] = znew
    scalnew_ref[...] = tile_of(alpha, gamma, pap, beta)
    send_faces(znew, columns_ref, msg_ref)


def second_of(right_ref, q_ref, v_ref, scal0_ref, scal_ref):
    image = v_ref[...] + scal_ref[3:4] * q_ref[...]
    return image, right_ref[...] - scal0_ref[0:1] * q_ref[...] - scal_ref[0:1] * image


def k_image2(
    recv_ref, z_ref, right_ref, q_ref, v_ref, scal0_ref, scal_ref, matrix_ref, rows_ref, columns_ref,
    image_ref, msg_ref,
):
    image = image_of(recv_ref, z_ref, matrix_ref, rows_ref, columns_ref)
    image_ref[...] = image
    z = z_ref[...]
    before, resid = second_of(right_ref, q_ref, v_ref, scal0_ref, scal_ref)
    aux = tile_of(rowdot(resid, z), rowdot(z, before), rowdot(z, image))
    msg_ref[...] = jnp.broadcast_to(aux[None, :4], LAST_GROUP)


def k_end(
    recv_ref, scal0_ref, scal_ref, z0_ref, z1_ref, z2_ref, right_ref, q_ref, v_ref, last_ref, xout_ref, rout_ref
):
    aux = jnp.sum(recv_ref[...], axis=0)
    gamma, cross, zaz = aux[0:1], aux[1:2], aux[2:3]
    beta = gamma / scal_ref[1:2]
    pap = zaz + beta * (2.0 * cross + beta * scal_ref[2:3])
    alpha = gamma / pap
    z0 = z0_ref[...]
    direction = z1_ref[...] + scal_ref[3:4] * z0
    x = scal0_ref[0:1] * z0 + scal_ref[0:1] * direction
    xout_ref[...] = x + alpha * (z2_ref[...] + beta * direction)
    image, resid = second_of(right_ref, q_ref, v_ref, scal0_ref, scal_ref)
    rout_ref[...] = resid - alpha * (last_ref[...] + beta * image)


class Far:
    def __init__(self, array):
        self.array = array


def call(kernel, outs, *args, smem=0, scratch=(), flops=1e6, far=()):
    near = pl.BlockSpec(memory_space=pltpu.VMEM)
    specs = [pl.BlockSpec(memory_space=pltpu.SMEM)] * smem
    specs += [pl.BlockSpec() if isinstance(a, Far) else near for a in args[smem:]]
    args = [pltpu.with_memory_space_constraint(a.array, pltpu.HBM) if isinstance(a, Far) else a for a in args]
    single = not isinstance(outs, list)
    sizes = [jax.ShapeDtypeStruct(s, d) for s, d in ([outs] if single else outs)]
    shapes = [pltpu.HBM(a.shape, a.dtype) if i in far else a for i, a in enumerate(sizes)]
    moved = sum(a.size * a.dtype.itemsize for a in [*args, *sizes])
    out = pl.pallas_call(
        kernel,
        out_shape=shapes,
        in_specs=specs,
        out_specs=[pl.BlockSpec() if i in far else near for i in range(len(shapes))],
        scratch_shapes=list(scratch),
        compiler_params=pltpu.CompilerParams(vmem_limit_bytes=24 << 20),
        cost_estimate=pl.CostEstimate(flops=int(flops), bytes_accessed=int(moved), transcendentals=0),
    )(*args)
    return out[0] if single else out


def swap(x, axis):
    order = [ORDER] if axis == "sub" else None
    return lax.all_to_all(x, axis, split_axis=0, concat_axis=0, tiled=True, axis_index_groups=order)


def local(
    right_side,
    mass,
    block_values,
    block_cols,
    face_rows,
    land_rows,
    face_counts,
    face_weight,
    local_factor,
    basis,
    coarse_inverse,
):
    vec = (VEC, F32)
    tile = ((8, RHS), F32)
    to_group, to_sub, to_face = (MSG_GROUP, F32), (MSG_SUB, F32), (MSG_FACE, F32)

    part, rows, columns = call(
        k_first,
        [to_group, ((8, SLOTS), F32), ((SLOTS, 128), F32)],
        Far(right_side),
        Far(basis),
        Far(face_rows),
        Far(land_rows),
        Far(face_counts),
        Far(face_weight),
    )
    part = swap(part, "group")
    whole = swap(call(k_gather_first, to_sub, part, columns), "sub")
    blocks, base = call(
        k_setup,
        [((ROWS, ROWS), F32), vec],
        block_cols,
        Far(block_values),
        Far(mass),
        smem=1,
        scratch=[pltpu.VMEM((ROWS, ROWS), F32)],
        far=(0, 1),
    )
    first_inverse, base = lax.optimization_barrier((coarse_inverse, base))
    solved = swap(call(k_solve, to_group, whole, first_inverse), "group")
    matrix, smoother = call(
        k_finish,
        [((ROWS, ROWS), F32), vec],
        whole,
        rows,
        columns,
        Far(base),
        Far(blocks),
        Far(local_factor),
    )

    def coarse(msg):
        whole = swap(call(k_gather, to_sub, swap(msg, "group")), "sub")
        return swap(call(k_solve, to_group, whole, coarse_inverse), "group")

    z0, msg = call(k_start, [vec, to_face], solved, right_side, smoother, basis, columns)
    q0, msg = call(
        k_image0, [vec, to_group], swap(msg, "sub"), z0, right_side, matrix, rows, columns, basis
    )
    u0, z1, scal0, msg = call(
        k_step0, [vec, vec, tile, to_face], coarse(msg), q0, smoother, z0, basis, columns
    )
    v1, msg = call(
        k_image1,
        [vec, to_group],
        swap(msg, "sub"),
        z1,
        right_side,
        q0,
        scal0,
        matrix,
        rows,
        columns,
        basis,
    )
    z2, scal1, msg = call(
        k_step1, [vec, tile, to_face], coarse(msg), v1, smoother, u0, z1, scal0, basis, columns
    )
    v2, msg = call(
        k_image2,
        [vec, (LAST_GROUP, F32)],
        swap(msg, "sub"),
        z2,
        right_side,
        q0,
        v1,
        scal0,
        scal1,
        matrix,
        rows,
        columns,
    )
    whole = swap(call(k_gather, (LAST_SUB, F32), swap(msg, "group")), "sub")
    return tuple(
        call(k_end, [vec, vec], whole, scal0, scal1, z0, z1, z2, right_side, q0, v1, v2)
    )


def solution(mesh):
    both = P(("group", "sub"), None)
    return jax.shard_map(
        local,
        mesh=mesh,
        in_specs=(both,) * 10 + (P("sub", None),),
        out_specs=(both, both),
        check_vma=False,
    )
```
